512 devices in a mesh: gx: 16 (over y, core), gy: 32 (over x, z).
Axes of the slice: x: 4, y: 8, z: 8, core: 2. Of those that a mesh axis runs over, the one named last changes fastest.
Arguments:
- stencil: bfloat16 [32, 128, 2, 64, 448], P('gx', 'gy')
- inverse_blocks: bfloat16 [32, 128, 64, 128], P('gx', 'gy')
- tentative: bfloat16 [32, 128, 8, 128], P('gx', 'gy'), may hold values from -0.75 to 0.75
- aggregate: int32 [32, 128, 2], P('gx', 'gy'), may hold values from 0 to 7
- fine_residual: float32 [32, 128, 128], P('gx', 'gy'), may hold values from -6 to 6
Outputs:
- coarse: float32 [16, 32, 128, 800], P('gx', 'gy')
- restricted: float32 [16, 32, 64], P('gx', 'gy')
The draws below stay inside these ranges and needn't reach their ends.
Inputs may be any that keep to these rules, and one draw needn't show every extreme that they name: aggregate numbers are local to the element's patch.
All inputs are finite; a program needn't handle non-finite values.
Results may differ from the reference program's by a relative error of at most 0.004.
Values may be sent and summed in bfloat16 or wider, within the bound.
A program may use at most 64 MiB of HBM per device.

```python
import math
import jax
import jax.numpy as jnp
from jax import lax

EDOF = 64
MODES = 8
AGG = 8
EX = 2
EY = 4
EZ = 2
NX = 32
NY = 128
NC = 64
HALF = 800
N_GX = 16
N_GY = 32


def draw_stencil(key, part):
    key = jax.random.fold_in(key, 11)
    first_key = jax.random.fold_in(key, 0)
    shape = (NX, NY, EZ, EDOF, 7 * EDOF)
    noise = jax.random.uniform(first_key, shape, jnp.float32, -1.0, 1.0)
    column = lax.broadcasted_iota(jnp.int32, shape, 4)
    row_place = lax.broadcasted_iota(jnp.int32, shape, 3)
    diagonal = jnp.where(row_place == column, 2.0, 0.0)
    inner = noise * (0.4 / math.sqrt(EDOF)) + diagonal
    faces = noise * (0.8 / math.sqrt(EDOF))
    return jnp.where(column < EDOF, inner, faces).astype(jnp.bfloat16)


def draw_inverse_blocks(key, part):
    key = jax.random.fold_in(key, 12)
    shape = (NX, NY, EDOF, EZ * EDOF)
    noise = jax.random.uniform(key, shape, jnp.float32, -1.0, 1.0)
    column = lax.broadcasted_iota(jnp.int32, shape, 3) % EDOF
    row_place = lax.broadcasted_iota(jnp.int32, shape, 2)
    scale = 0.3 / math.sqrt(EDOF)
    return (jnp.where(row_place == column, 0.4, 0.0) + noise * scale).astype(jnp.bfloat16)


def place_ends(values, own_key, low, largest):
    index_at = [jax.random.randint(jax.random.fold_in(own_key, axis), (), 0, length) for axis, length in enumerate(values.shape)]
    longest = values.shape.index(max(values.shape))
    beside = index_at[:longest] + [(index_at[longest] + 1) % values.shape[longest]] + index_at[longest + 1:]
    return values.at[tuple(index_at)].set(low).at[tuple(beside)].set(largest)


def level_of(rng, dims, shards, low, top_value):
    factor_of = 1.0
    for dim, blocks in shards:
        steps = jax.random.uniform(jax.random.fold_in(jax.random.fold_in(rng, 6), dim), (blocks,), jnp.float32, low / len(shards), top_value / len(shards))
        factor_of = factor_of * jnp.repeat(jnp.exp(steps), dims[dim] // blocks).reshape((-1,) + (1,) * (len(dims) - 1 - dim))
    return factor_of


def centred(own_key, extent, scale, bound, shards=(), kind=jnp.bfloat16):
    level = level_of(own_key, extent, shards, -0.22, 0.18) if shards else 1.0
    values = jax.random.normal(own_key, extent, jnp.float32) * scale * level
    return jnp.minimum(jnp.maximum(values, -bound), bound).astype(kind)


def setup_inputs(seed: int = 0) -> dict:
    key_of = jax.random.split(jax.random.key(seed), 6)
    stencil = draw_stencil(jax.random.fold_in(key_of[5], 71), 0)
    inverse_blocks = draw_inverse_blocks(jax.random.fold_in(key_of[5], 71), 0)
    tentative = centred(key_of[2], (NX, NY, MODES, EZ * EDOF), EDOF ** -0.5, 0.75, ((0, 16), (1, 32)))
    aggregate = place_ends(jax.random.randint(key_of[3], (NX, NY, EZ), 0, AGG), jax.random.fold_in(key_of[3], 1), 0, AGG - 1).astype(jnp.int32)
    fine_residual = centred(key_of[4], (NX, NY, EZ * EDOF), 1.0, 6.0, ((0, 16), (1, 32)), jnp.float32)
    return {"stencil": stencil, "inverse_blocks": inverse_blocks, "tentative": tentative, "aggregate": aggregate, "fine_residual": fine_residual}


relax_weight = 0.6
SINGLE_FRAME = [(0, 0)]
NEAR_FRAME = [(0, 0), (-1, 0), (1, 0), (0, -1), (0, 1)]
MIDDLE_FRAME = [(across, offset) for across in range(-2, 3) for offset in range(-2, 3) if abs(across) + abs(offset) <= 2]
OUTER_FRAME = [(across, offset) for across in range(-3, 4) for offset in range(-3, 4) if abs(across) + abs(offset) <= 3]
DIRECTIONS = [(0, 0, 0), (-1, 0, 0), (1, 0, 0), (0, -1, 0), (0, 1, 0), (0, 0, -1), (0, 0, 1)]


def build_seed(tentative, aggregate):
    xcount, ycount, zcount = aggregate.shape
    mode_count = tentative.shape[2]
    block_size = tentative.shape[3] // zcount
    member = aggregate[..., None] == jnp.arange(AGG, dtype=jnp.int32)
    modal_rows = tentative.reshape(xcount, ycount, mode_count, zcount, block_size).transpose(0, 1, 3, 4, 2)
    seed_rows = jnp.where(member[:, :, :, None, :, None], modal_rows[:, :, :, :, None, :], jnp.zeros((), tentative.dtype))
    return seed_rows.reshape(xcount, ycount, zcount, block_size, AGG * mode_count)


def couple(stencil, extended, inner_frame, outer_frame):
    xcount, ycount, zcount, block_size = stencil.shape[:4]
    column_width = extended.shape[-1] // len(inner_frame)
    xplace = lax.broadcasted_iota(jnp.int32, (xcount, ycount, zcount, 1, 1), 0)
    yplace = lax.broadcasted_iota(jnp.int32, (xcount, ycount, zcount, 1, 1), 1)
    slot_sums = [jnp.zeros((xcount, ycount, zcount, block_size, column_width), jnp.float32) for target in outer_frame]
    for direction, (step_x, step_y, step_z) in enumerate(DIRECTIONS):
        coupling = stencil[:, :, :, :, direction * block_size:(direction + 1) * block_size]
        nearby = extended[1 + step_x:1 + step_x + xcount, 1 + step_y:1 + step_y + ycount, 1 + step_z:1 + step_z + zcount]
        product_term = jnp.einsum('xyzij,xyzjc->xyzic', coupling.astype(jnp.float32), nearby.astype(jnp.float32), precision=lax.Precision.HIGHEST)
        if step_x != 0 or step_y != 0:
            if step_x == -1:
                crossing = xplace == 0
            elif step_x == 1:
                crossing = xplace == xcount - 1
            elif step_y == -1:
                crossing = yplace == 0
            else:
                crossing = yplace == ycount - 1
            placements = [((0, 0), jnp.logical_not(crossing)), ((step_x, step_y), crossing)]
        else:
            placements = [((0, 0), None)]
        for (move_x, move_y), allowed in placements:
            for position, (from_x, from_y) in enumerate(inner_frame):
                target = outer_frame.index((move_x + from_x, move_y + from_y))
                portion = product_term[..., position * column_width:(position + 1) * column_width]
                if allowed is not None:
                    portion = jnp.where(allowed, portion, jnp.zeros((), jnp.float32))
                slot_sums[target] = slot_sums[target] + portion
    return jnp.concatenate(slot_sums, axis=-1)


def smooth(stencil, inverse_blocks, seed_rows, seed_ext):
    xcount, ycount, zcount, block_size = stencil.shape[:4]
    applied = couple(stencil, seed_ext, SINGLE_FRAME, NEAR_FRAME).astype(jnp.bfloat16)
    inverse = inverse_blocks.reshape(xcount, ycount, block_size, zcount, block_size)
    relaxed = jnp.einsum('xyizj,xyzjc->xyzic', inverse.astype(jnp.float32), applied.astype(jnp.float32), precision=lax.Precision.HIGHEST)
    padding = jnp.zeros(seed_rows.shape[:4] + (4 * seed_rows.shape[4],), jnp.float32)
    seeded = jnp.concatenate([seed_rows.astype(jnp.float32), padding], axis=-1)
    return (seeded - relax_weight * relaxed).astype(jnp.bfloat16)


def galerkin(stencil, prolong, prolong_ext, fine_residual):
    coupled = couple(stencil, prolong_ext, NEAR_FRAME, MIDDLE_FRAME).astype(jnp.bfloat16)
    row_count = prolong.shape[0] * prolong.shape[1] * prolong.shape[2] * prolong.shape[3]
    left_rows = prolong.reshape(row_count, -1).astype(jnp.float32)
    right_rows = coupled.reshape(row_count, -1).astype(jnp.float32)
    contribution = lax.dot_general(left_rows, right_rows, (((0,), (0,)), ((), ())), precision=lax.Precision.HIGHEST)
    restrict_terms = lax.dot_general(left_rows, fine_residual.reshape(row_count), (((0,), (0,)), ((), ())), precision=lax.Precision.HIGHEST)
    return contribution, restrict_terms


def local_patch(array, patch, extra):
    start_x = ((patch // N_GY) * EX).astype(jnp.int32)
    start_y = ((patch % N_GY) * EY).astype(jnp.int32)
    starts = (start_x, start_y) + tuple(jnp.zeros((), jnp.int32) for other in array.shape[2:])
    return lax.dynamic_slice(array, starts, (EX + extra, EY + extra) + array.shape[2:])


def from_sender(array, off_x, off_y):
    padded = jnp.pad(array, ((1, 1), (1, 1)) + tuple((0, 0) for other in array.shape[2:]))
    return padded[1 - off_x:1 - off_x + N_GX, 1 - off_y:1 - off_y + N_GY]


def reference(stencil, inverse_blocks, tentative, aggregate, fine_residual):
    seed_rows = build_seed(tentative, aggregate)
    seed_pad = jnp.pad(seed_rows, ((1, 1), (1, 1), (1, 1), (0, 0), (0, 0)))
    patches = jnp.arange(N_GX * N_GY, dtype=jnp.int32)

    def smooth_patch(patch):
        return smooth(local_patch(stencil, patch, 0), local_patch(inverse_blocks, patch, 0), local_patch(seed_rows, patch, 0), local_patch(seed_pad, patch, 2))

    prolong_parts = lax.map(smooth_patch, patches)
    prolong = prolong_parts.reshape(N_GX, N_GY, EX, EY, EZ, EDOF, 5 * NC).transpose(0, 2, 1, 3, 4, 5, 6).reshape(NX, NY, EZ, EDOF, 5 * NC)
    prolong_pad = jnp.pad(prolong, ((1, 1), (1, 1), (1, 1), (0, 0), (0, 0)))

    def galerkin_patch(patch):
        return galerkin(local_patch(stencil, patch, 0), local_patch(prolong, patch, 0), local_patch(prolong_pad, patch, 2), local_patch(fine_residual, patch, 0))

    contributions, restrict_terms = lax.map(galerkin_patch, patches)
    contributions = contributions.reshape(N_GX, N_GY, 5 * NC, 13 * NC)
    restrict_terms = restrict_terms.reshape(N_GX, N_GY, 5 * NC)
    slot_sums = [jnp.zeros((N_GX, N_GY, NC, NC), jnp.float32) for target in OUTER_FRAME]
    restricted = jnp.zeros((N_GX, N_GY, NC), jnp.float32)
    for position, (off_x, off_y) in enumerate(NEAR_FRAME):
        arrived = from_sender(contributions[:, :, position * NC:(position + 1) * NC, :], off_x, off_y)
        restricted = restricted + from_sender(restrict_terms[:, :, position * NC:(position + 1) * NC], off_x, off_y)
        for column, (col_x, col_y) in enumerate(MIDDLE_FRAME):
            target = OUTER_FRAME.index((col_x - off_x, col_y - off_y))
            slot_sums[target] = slot_sums[target] + arrived[..., column * NC:(column + 1) * NC]
    assembled = jnp.concatenate(slot_sums, axis=-1)
    paired = assembled.reshape(N_GX // 2, 2, N_GY, NC, 2, HALF).transpose(0, 4, 2, 1, 3, 5)
    coarse = paired.reshape(N_GX, N_GY, 2 * NC, HALF)
    return coarse, restricted
```

```python
import jax
import jax.numpy as jnp
from jax import lax
from jax.experimental import pallas as pl
from jax.experimental.pallas import tpu as pltpu
from jax.sharding import PartitionSpec as P

MESH = pl.DeviceIdType.MESH
F32, BF16 = jnp.float32, jnp.bfloat16
AGG = 8
MODES = 8
RELAX = 0.6


X_AT, Y_AT = (0, 2, 3, 4), {0: 1, 3: 5}


def nt(left, right):
    return lax.dot_general(left, right, (((1,), (1,)), ((), ())), preferred_element_type=F32)


def expand(tile):
    values, code = tile[0:MODES].astype(F32), tile[MODES : 2 * MODES].astype(F32)
    rows = [jnp.where(code == float(a), values, 0.0) for a in range(AGG)]
    return jnp.concatenate(rows, axis=0).astype(BF16)


def swap(tile):
    return pltpu.roll(tile, 64, 1)


def kernel(
    n_gx,
    n_gy,
    stencil,
    inverse,
    tentative,
    aggregate,
    residual,
    out,
    restricted,
    sten_v,
    inv_v,
    tent_v,
    agg_v,
    res_v,
    w_v,
    wb_v,
    pack_v,
    hx_v,
    hy_v,
    p0_v,
    hp0x_v,
    hp0y_v,
    pc_v,
    hpcx_v,
    hpcy_v,
    st_v,
    lx_v,
    acc_v,
    snd_v,
    rcv_v,
    load_sem,
    send_sem,
    recv_sem,
):
    gx, gy = lax.axis_index("gx"), lax.axis_index("gy")
    odd = lax.rem(gx, 2)
    is_odd = odd == 1
    turn = 2 * odd - 1
    partner = gx - turn
    outer = lax.rem(gx + turn + n_gx, n_gx)
    outer2 = lax.rem(gx + 2 * turn + n_gx, n_gx)
    back2 = lax.rem(gx - 2 * turn + n_gx, n_gx)
    below = lax.rem(gy - 1 + n_gy, n_gy)
    above = lax.rem(gy + 1, n_gy)
    has_outer = jnp.logical_and(gx > 0, gx < n_gx - 1)
    has_below, has_above = gy > 0, gy < n_gy - 1

    loads = []

    def load(src, dst):
        copy = pltpu.make_async_copy(src, dst, load_sem.at[len(loads)])
        copy.start()
        loads.append(copy)
        return copy

    small = []
    for side in range(2):
        x = side + odd - 2 * side * odd
        small.append(load(tentative.at[x], tent_v.at[side]))
        small.append(load(aggregate.at[x], agg_v.at[side]))
    big = []
    for side in range(2):
        x = side + odd - 2 * side * odd
        big.append(load(stencil.at[x], sten_v.at[side]))
        big.append(load(inverse.at[x], inv_v.at[side]))
        big.append(load(residual.at[x], res_v.at[side]))

    barrier = pltpu.get_barrier_semaphore()
    peers = [
        (partner, gy),
        (outer, gy),
        (outer2, gy),
        (back2, gy),
        (gx, below),
        (gx, above),
        (partner, below),
        (partner, above),
    ]
    for peer in peers:
        pl.semaphore_signal(barrier, inc=1, device_id=peer, device_id_type=MESH)

    sends = []

    def send(src, dst, peer):
        at = len(sends)
        copy = pltpu.make_async_remote_copy(
            src_ref=src,
            dst_ref=dst,
            send_sem=send_sem.at[at],
            recv_sem=recv_sem.at[at],
            device_id=peer,
            device_id_type=MESH,
        )
        copy.start()
        sends.append(copy)
        return copy

    lane = lax.broadcasted_iota(jnp.int32, (8, 128), 1)
    for copy in small:
        copy.wait()
    for side in range(2):
        for y in range(4):
            code = jnp.where(
                lane < 64,
                jnp.broadcast_to(agg_v[side, y : y + 1, 0:1], (8, 128)),
                jnp.broadcast_to(agg_v[side, y : y + 1, 1:2], (8, 128)),
            )
            tile = jnp.concatenate([tent_v[side, y].astype(F32), code.astype(F32)], axis=0)
            pack_v[side, y] = tile.astype(BF16)

    pl.semaphore_wait(barrier, len(peers))
    seed_x = [
        send(pack_v.at[0], hx_v.at[0], (outer, gy)),
        send(pack_v.at[1], hx_v.at[1], (partner, gy)),
    ]
    seed_y = [
        send(pack_v.at[:, 0], hy_v.at[1], (gx, below)),
        send(pack_v.at[:, 3], hy_v.at[0], (gx, above)),
    ]

    for y in range(4):
        both = jnp.concatenate([pack_v[0, y], pack_v[1, y]], axis=1)
        st_v[y] = expand(both)

    for copy in big:
        copy.wait()
    wide = lax.broadcasted_iota(jnp.int32, (64, 128), 1)
    low = wide < 64
    zero = jnp.zeros((64, 128), F32)

    def put(kind, y, place, first, second):
        rows = pl.ds(place * 64, 64)
        w_v[y, kind, rows, 0:128] = first.astype(BF16)
        w_v[y, kind, rows, 128:256] = second.astype(BF16)

    for y in range(4):
        for side in range(2):
            inv = inv_v[side, y].astype(F32)
            for z in range(2):
                place = 2 * side + z
                block = jnp.where(low if z == 0 else jnp.logical_not(low), inv, 0.0)
                tiles = [block, zero] if side == 0 else [zero, block]
                wb_v[y, pl.ds(place * 64, 64), 0:128] = tiles[0].astype(BF16)
                wb_v[y, pl.ds(place * 64, 64), 128:256] = tiles[1].astype(BF16)

                a = sten_v[side, y, z, :, 0:128].astype(F32)
                b = sten_v[side, y, z, :, 128:256].astype(F32)
                c = sten_v[side, y, z, :, 256:384].astype(F32)
                d = sten_v[side, y, z, :, 384:448].astype(F32)
                d = jnp.concatenate([d, d], axis=1)
                ra, rb, rc = swap(a), swap(b), swap(c)
                if z == 0:
                    own = jnp.where(low, a, d)
                    toward_o, toward_i = jnp.where(is_odd, b, ra), jnp.where(is_odd, ra, b)
                    toward_m, toward_p = rb, c
                    keep = low
                else:
                    own = jnp.where(low, rc, ra)
                    toward_o, toward_i = jnp.where(is_odd, rb, a), jnp.where(is_odd, a, rb)
                    toward_m, toward_p = b, rc
                    keep = jnp.logical_not(low)
                toward_o = jnp.where(keep, toward_o, 0.0)
                toward_i = jnp.where(keep, toward_i, 0.0)
                toward_m = jnp.where(keep, toward_m, 0.0)
                toward_p = jnp.where(keep, toward_p, 0.0)
                if y == 0:
                    toward_m = jnp.where(has_below, toward_m, 0.0)
                if y == 3:
                    toward_p = jnp.where(has_above, toward_p, 0.0)
                if side == 0:
                    put(0, y, place, own, toward_i)
                    put(1, y, place, jnp.where(has_outer, toward_o, 0.0), zero)
                    put(2, y, place, toward_m, zero)
                    put(3, y, place, toward_p, zero)
                else:
                    put(0, y, place, toward_o, own)
                    put(1, y, place, zero, toward_i)
                    put(2, y, place, zero, toward_m)
                    put(3, y, place, zero, toward_p)

    def first_slot(y):
        applied = nt(st_v[y], w_v[y, 0])
        if y > 0:
            applied = applied + nt(st_v[y - 1], w_v[y, 2])
        if y < 3:
            applied = applied + nt(st_v[y + 1], w_v[y, 3])
        relaxed = nt(applied.astype(BF16), wb_v[y])
        p0_v[y] = (st_v[y].astype(F32) - RELAX * relaxed).astype(BF16)

    first_slot(0)
    first_y = [send(p0_v.at[0], hp0y_v.at[1], (gx, below))]
    first_slot(3)
    first_y.append(send(p0_v.at[3], hp0y_v.at[0], (gx, above)))
    first_slot(1)
    first_slot(2)
    first_x = [
        send(p0_v.at[:, :, 0:128], hp0x_v.at[:, :, 0:128], (outer, gy)),
        send(p0_v.at[:, :, 128:256], hp0x_v.at[:, :, 128:256], (partner, gy)),
    ]

    for copy in seed_x + seed_y:
        copy.wait_recv()

    def side_slots(y):
        halo = jnp.concatenate([hx_v[0, y], hx_v[1, y]], axis=1)
        halos, applied = [halo], [nt(halo, w_v[y, 1]).astype(BF16)]
        if y in (0, 3):
            end = 0 if y == 0 else 1
            halo = jnp.concatenate([hy_v[end, 0], hy_v[end, 1]], axis=1)
            halos.append(halo)
            applied.append(nt(halo, w_v[y, 2 + end]).astype(BF16))
        applied = applied[0] if len(applied) == 1 else jnp.concatenate(applied, axis=0)
        relaxed = nt(applied, wb_v[y])
        for n, at in enumerate([X_AT[y]] + ([Y_AT[y]] if y in Y_AT else [])):
            values = -RELAX * relaxed[16 * n : 16 * n + MODES]
            tile = jnp.concatenate([values, halos[n][MODES:].astype(F32)], axis=0)
            pc_v[at] = tile.astype(BF16)

    side_slots(0)
    side_slots(3)
    side_y = [
        send(pc_v.at[0:2], hpcy_v.at[1], (gx, below)),
        send(pc_v.at[4:6], hpcy_v.at[0], (gx, above)),
    ]
    side_slots(1)
    side_slots(2)
    side_x = [
        send(pc_v.at[:, :, 0:128], hpcx_v.at[:, :, 0:128], (outer, gy)),
        send(pc_v.at[:, :, 128:256], hpcx_v.at[:, :, 128:256], (partner, gy)),
    ]

    out[...] = jnp.zeros(out.shape, F32)
    blank = jnp.zeros((64, 128), BF16)
    for y in range(4):
        full = expand(pc_v[X_AT[y]])
        lx_v[y, 0:64, 0:128] = full[:, 0:128]
        lx_v[y, 0:64, 128:256] = blank
        lx_v[y, 64:128, 0:128] = blank
        lx_v[y, 64:128, 128:256] = full[:, 128:256]
        if y in Y_AT:
            lx_v[y, 128:192] = expand(pc_v[Y_AT[y]])

    def left(y, rows):
        return jnp.concatenate([p0_v[y], lx_v[y, 0 : rows - 64]], axis=0)

    terms = [jnp.zeros((64, 1), F32) for slot in range(5)]
    for y in range(4):
        res = jnp.concatenate([res_v[0, y : y + 1, :], res_v[1, y : y + 1, :]], axis=1)
        blocks = [(0, p0_v[y]), (1, lx_v[y, 0:64]), (2, lx_v[y, 64:128])]
        if y in Y_AT:
            blocks.append((3 if y == 0 else 4, lx_v[y, 128:192]))
        for slot, block in blocks:
            terms[slot] = terms[slot] + jnp.sum(block.astype(F32) * res, axis=1, keepdims=True)

    for y in range(4):
        size = 256 if y in Y_AT else 192
        acc_v[y, 0:size] = nt(left(y, size), w_v[y, 0])
        if y not in Y_AT:
            acc_v[y, 192:256] = jnp.zeros((64, 256), F32)
        if y > 0:
            size = 256 if y - 1 in Y_AT else 192
            acc_v[y, 0:size] = acc_v[y, 0:size] + nt(left(y - 1, size), w_v[y, 2])
        if y < 3:
            size = 256 if y + 1 in Y_AT else 192
            acc_v[y, 0:size] = acc_v[y, 0:size] + nt(left(y + 1, size), w_v[y, 3])

    for copy in first_x + first_y:
        copy.wait_recv()
    for y in range(4):
        part = nt(hp0x_v[y], w_v[y, 1])
        acc_v[y, 64:128, 0:128] = acc_v[y, 64:128, 0:128] + part[:, 0:128]
        acc_v[y, 128:192, 128:256] = acc_v[y, 128:192, 128:256] + part[:, 128:256]
        if y in Y_AT:
            end = 0 if y == 0 else 1
            acc_v[y, 192:256] = acc_v[y, 192:256] + nt(hp0y_v[end], w_v[y, 2 + end])

    for copy in side_y + side_x:
        copy.wait_recv()

    def finish(y):
        if y in Y_AT:
            end = 0 if y == 0 else 1
            fromx = jnp.concatenate([expand(hpcx_v[X_AT[y]]), expand(hpcx_v[Y_AT[y]])], axis=0)
            partx = nt(fromx, w_v[y, 1])
            fromy = jnp.concatenate([expand(hpcy_v[end, 0]), expand(hpcy_v[end, 1])], axis=0)
            party = nt(fromy, w_v[y, 2 + end])
            own = (acc_v[y, 0:64] + partx[0:64] + party[64:128]).astype(BF16)
            corner = (partx[64:128] + party[0:64]).astype(BF16)
            mid = acc_v[y, 64:256].astype(BF16)
            corner_o = jnp.concatenate([corner[:, 0:128], blank], axis=1)
            corner_i = jnp.concatenate([blank, corner[:, 128:256]], axis=1)
            right = jnp.concatenate(
                [own, mid[128:192], corner_o, mid[0:64], corner_i, mid[64:128]], axis=0
            )
            return nt(left(y, 256), right)
        partx = nt(expand(hpcx_v[X_AT[y]]), w_v[y, 1])
        own = (acc_v[y, 0:64] + partx).astype(BF16)
        mid = acc_v[y, 64:256].astype(BF16)
        right = jnp.concatenate([own, mid[128:192], mid[64:128], mid[0:64]], axis=0)
        return nt(left(y, 192), right)

    def pick(first, second):
        return jnp.where(low, first, second)

    def half(tile, near):
        moved = jnp.where(low, tile, pltpu.roll(tile, 96, 1))
        return jnp.where(is_odd, moved, tile) if near else jnp.where(is_odd, tile, moved)

    def with_terms(tile, term):
        upper = term.astype(BF16).astype(F32)
        return jnp.where(wide == 96, upper, jnp.where(wide == 97, term - upper, tile))

    def tiles(product, slot):
        rows = product[slot * 64 : slot * 64 + 64]
        return [rows[:, 128 * t : 128 * t + 128] for t in range(rows.shape[1] // 128)]

    def post(at, values):
        for n, value in enumerate(values):
            snd_v[at + n] = value.astype(BF16)

    g0 = finish(0)
    t0, t1, t2 = tiles(g0, 3)
    post(8, [with_terms(half(pick(jnp.where(is_odd, t0, 0.0), t0), True), terms[3]), t1])
    post(10, [half(pick(jnp.where(is_odd, 0.0, t0), t0), False), t2])
    msgs = [
        send(snd_v.at[8:10], rcv_v.at[8:10], (gx, below)),
        send(snd_v.at[10:12], rcv_v.at[10:12], (partner, below)),
    ]
    g3 = finish(3)
    t0, t1, t2 = tiles(g3, 3)
    post(12, [with_terms(half(pick(jnp.where(is_odd, 0.0, t0), t0), True), terms[4]), t1])
    post(14, [half(pick(jnp.where(is_odd, t0, 0.0), t0), False), t2])
    msgs += [
        send(snd_v.at[12:14], rcv_v.at[12:14], (gx, above)),
        send(snd_v.at[14:16], rcv_v.at[14:16], (partner, above)),
    ]
    g1 = finish(1)
    g2 = finish(2)

    def summed(slot):
        a0, a1, a2 = tiles(g0, slot)
        b0, b1, b2 = tiles(g3, slot)
        c0, c1 = tiles(g1, slot)
        d0, d1 = tiles(g2, slot)
        um, up = a0 + c0, b0 + d0
        mid = c1 + d1
        return um, up, um + up, a1, b1, a1 + b1 + mid, a2, b2, a2 + b2 + swap(mid)

    def by_side(first, second):
        return jnp.where(is_odd, second, first)

    um, up, mid, om, op, o_sum, im, ip, i_sum = summed(1)
    post(
        4,
        [
            with_terms(half(pick(by_side(op, om), o_sum), False), terms[1]),
            pick(mid, up),
            pick(swap(um), i_sum),
        ],
    )
    post(7, [half(pick(by_side(om, op), o_sum), True)])
    msgs += [
        send(snd_v.at[4:7], rcv_v.at[4:7], (outer, gy)),
        send(snd_v.at[7:8], rcv_v.at[7:8], (outer2, gy)),
    ]
    um, up, mid, om, op, o_sum, im, ip, i_sum = summed(2)
    post(3, [with_terms(half(pick(by_side(ip, im), i_sum), False), terms[2])])
    far_a = half(pick(by_side(im, ip), i_sum), True)
    far_b = pick(mid, up)
    far_c = pick(swap(um), o_sum)
    um, up, mid, om, op, o_sum, im, ip, i_sum = summed(0)
    post(
        0,
        [
            half(swap(pick(mid, by_side(up, um))), False),
            swap(pick(ip, i_sum)),
            pick(im, 0.0),
        ],
    )
    msgs += [send(snd_v.at[0:4], rcv_v.at[0:4], (partner, gy))]
    own_a = with_terms(half(swap(pick(mid, by_side(um, up))), True), terms[0])
    own_b = swap(pick(op, o_sum))
    own_c = pick(om, 0.0)

    for copy in msgs:
        copy.wait_recv()

    def got(at):
        return rcv_v[at].astype(F32)

    y_near, y_far = got(13), got(15)
    own_a = own_a + got(3) + got(4) + got(8) + got(12)
    own_b = own_b + got(5) + got(9) + pick(y_near, 0.0)
    own_c = own_c + got(6) + pick(swap(y_near), 0.0)
    far_a = far_a + got(0) + got(7) + got(10) + got(14)
    far_b = far_b + got(1) + got(11) + pick(y_far, 0.0)
    far_c = far_c + got(2) + pick(swap(y_far), 0.0)

    @pl.when(odd == 0)
    def _():
        for row, (a, b, c) in enumerate([(own_a, own_b, own_c), (far_a, far_b, far_c)]):
            rows = pl.ds(row * 64, 64)
            ra, rc = swap(a), swap(c)
            out[0, 0, rows, 128:256] = pick(rc, 0.0)
            out[0, 0, rows, 256:384] = pick(0.0, rc)
            out[0, 0, rows, 384:512] = b
            out[0, 0, rows, 640:768] = pick(0.0, ra)
            out[0, 0, rows, 768:800] = ra[:, 0:32]

    @pl.when(odd == 1)
    def _():
        for row, (a, b, c) in enumerate([(far_a, far_b, far_c), (own_a, own_b, own_c)]):
            rows = pl.ds(row * 64, 64)
            ra, ta = swap(a), pltpu.roll(a, 32, 1)
            tb, tc = pltpu.roll(b, 96, 1), pltpu.roll(c, 32, 1)
            out[0, 0, rows, 0:128] = jnp.where(wide < 32, ra, jnp.where(wide < 96, ta, 0.0))
            out[0, 0, rows, 256:384] = jnp.where(
                wide < 32, 0.0, jnp.where(wide < 96, tc, tb)
            )
            out[0, 0, rows, 384:512] = jnp.where(wide < 96, tb, 0.0)
            out[0, 0, rows, 512:640] = jnp.where(wide < 96, 0.0, tc)
            out[0, 0, rows, 640:768] = jnp.where(wide < 32, tc, 0.0)

    turned = own_a.T
    restricted[0] = turned[96:97, :] + turned[97:98, :]

    for copy in sends:
        copy.wait_send()


def body(stencil, inverse, tentative, aggregate, residual):
    any_space = pl.BlockSpec(memory_space=pl.ANY)
    vmem = pl.BlockSpec(memory_space=pltpu.VMEM)
    scratch = [
        pltpu.VMEM(stencil.shape, BF16),
        pltpu.VMEM(inverse.shape, BF16),
        pltpu.VMEM(tentative.shape, BF16),
        pltpu.VMEM(aggregate.shape, jnp.int32),
        pltpu.VMEM(residual.shape, F32),
        pltpu.VMEM((4, 4, 256, 256), BF16),
        pltpu.VMEM((4, 256, 256), BF16),
        pltpu.VMEM((2, 4, 16, 128), BF16),
        pltpu.VMEM((2, 4, 16, 128), BF16),
        pltpu.VMEM((2, 2, 16, 128), BF16),
        pltpu.VMEM((4, 64, 256), BF16),
        pltpu.VMEM((4, 64, 256), BF16),
        pltpu.VMEM((2, 64, 256), BF16),
        pltpu.VMEM((6, 16, 256), BF16),
        pltpu.VMEM((6, 16, 256), BF16),
        pltpu.VMEM((2, 2, 16, 256), BF16),
        pltpu.VMEM((4, 64, 256), BF16),
        pltpu.VMEM((4, 192, 256), BF16),
        pltpu.VMEM((4, 256, 256), F32),
        pltpu.VMEM((16, 64, 128), BF16),
        pltpu.VMEM((16, 64, 128), BF16),
        pltpu.SemaphoreType.DMA((10,)),
        pltpu.SemaphoreType.DMA((19,)),
        pltpu.SemaphoreType.DMA((19,)),
    ]
    sizes = (lax.axis_size("gx"), lax.axis_size("gy"))

    def call(*refs):
        kernel(*sizes, *refs)

    return pl.pallas_call(
        call,
        out_shape=(
            jax.ShapeDtypeStruct((1, 1, 128, 800), F32),
            jax.ShapeDtypeStruct((1, 1, 64), F32),
        ),
        in_specs=[any_space] * 5,
        out_specs=(vmem, vmem),
        scratch_shapes=scratch,
        compiler_params=pltpu.CompilerParams(
            collective_id=0, has_side_effects=True, vmem_limit_bytes=32 << 20
        ),
        name="galerkin",
    )(stencil, inverse, tentative, aggregate, residual)


def solution(mesh):
    in_specs = (
        P("gx", "gy", None, None, None),
        P("gx", "gy", None, None),
        P("gx", "gy", None, None),
        P("gx", "gy", None),
        P("gx", "gy", None),
    )
    out_specs = (P("gx", "gy", None, None), P("gx", "gy", None))
    return jax.shard_map(body, mesh=mesh, in_specs=in_specs, out_specs=out_specs, check_vma=False)
```

```python
import jax
import jax.numpy as jnp
from jax import lax
from jax.experimental import pallas as pl
from jax.experimental.pallas import tpu as pltpu
from jax.sharding import PartitionSpec as P

MESH = pl.DeviceIdType.MESH
F32, BF16 = jnp.float32, jnp.bfloat16
AGG = 8
MODES = 8
RELAX = 0.6


X_AT, Y_AT = (0, 2, 3, 4), {0: 1, 3: 5}


def nt(left, right):
    return lax.dot_general(left, right, (((1,), (1,)), ((), ())), preferred_element_type=F32)


def expand(tile):
    values, code = tile[0:MODES].astype(F32), tile[MODES : 2 * MODES].astype(F32)
    rows = [jnp.where(code == float(a), values, 0.0) for a in range(AGG)]
    return jnp.concatenate(rows, axis=0).astype(BF16)


def swap(tile):
    return pltpu.roll(tile, 64, 1)


def kernel(
    n_gx,
    n_gy,
    stencil,
    inverse,
    tentative,
    aggregate,
    residual,
    out,
    sten_v,
    inv_v,
    tent_v,
    agg_v,
    res_v,
    w_v,
    wb_v,
    pack_v,
    hx_v,
    hy_v,
    p0_v,
    hp0x_v,
    hp0y_v,
    pc_v,
    hpcx_v,
    hpcy_v,
    st_v,
    lx_v,
    acc_v,
    snd_v,
    rcv_v,
    load_sem,
    send_sem,
    recv_sem,
):
    gx, gy = lax.axis_index("gx"), lax.axis_index("gy")
    odd = lax.rem(gx, 2)
    is_odd = odd == 1
    turn = 2 * odd - 1
    partner = gx - turn
    outer = lax.rem(gx + turn + n_gx, n_gx)
    outer2 = lax.rem(gx + 2 * turn + n_gx, n_gx)
    back2 = lax.rem(gx - 2 * turn + n_gx, n_gx)
    below = lax.rem(gy - 1 + n_gy, n_gy)
    above = lax.rem(gy + 1, n_gy)
    has_outer = jnp.logical_and(gx > 0, gx < n_gx - 1)
    has_below, has_above = gy > 0, gy < n_gy - 1

    loads = []

    def load(src, dst):
        copy = pltpu.make_async_copy(src, dst, load_sem.at[len(loads)])
        copy.start()
        loads.append(copy)
        return copy

    small = []
    for side in range(2):
        x = side + odd - 2 * side * odd
        small.append(load(tentative.at[x], tent_v.at[side]))
        small.append(load(aggregate.at[x], agg_v.at[side]))
    big = []
    for side in range(2):
        x = side + odd - 2 * side * odd
        big.append(load(stencil.at[x], sten_v.at[side]))
        big.append(load(inverse.at[x], inv_v.at[side]))
        big.append(load(residual.at[x], res_v.at[side]))

    barrier = pltpu.get_barrier_semaphore()
    peers = [
        (partner, gy),
        (outer, gy),
        (outer2, gy),
        (back2, gy),
        (gx, below),
        (gx, above),
        (partner, below),
        (partner, above),
    ]
    for peer in peers:
        pl.semaphore_signal(barrier, inc=1, device_id=peer, device_id_type=MESH)

    sends = []

    def send(src, dst, peer):
        at = len(sends)
        copy = pltpu.make_async_remote_copy(
            src_ref=src,
            dst_ref=dst,
            send_sem=send_sem.at[at],
            recv_sem=recv_sem.at[at],
            device_id=peer,
            device_id_type=MESH,
        )
        copy.start()
        sends.append(copy)
        return copy

    lane = lax.broadcasted_iota(jnp.int32, (8, 128), 1)
    for copy in small:
        copy.wait()
    for side in range(2):
        for y in range(4):
            code = jnp.where(
                lane < 64,
                jnp.broadcast_to(agg_v[side, 0:1, y : y + 1], (8, 128)),
                jnp.broadcast_to(agg_v[side, 1:2, y : y + 1], (8, 128)),
            )
            tile = jnp.concatenate([tent_v[side, y].astype(F32), code.astype(F32)], axis=0)
            pack_v[side, y] = tile.astype(BF16)

    pl.semaphore_wait(barrier, len(peers))
    seed_x = [
        send(pack_v.at[0], hx_v.at[0], (outer, gy)),
        send(pack_v.at[1], hx_v.at[1], (partner, gy)),
    ]
    seed_y = [
        send(pack_v.at[:, 0], hy_v.at[1], (gx, below)),
        send(pack_v.at[:, 3], hy_v.at[0], (gx, above)),
    ]

    for y in range(4):
        both = jnp.concatenate([pack_v[0, y], pack_v[1, y]], axis=1)
        st_v[y] = expand(both)

    for copy in big:
        copy.wait()
    wide = lax.broadcasted_iota(jnp.int32, (64, 128), 1)
    low = wide < 64
    zero = jnp.zeros((64, 128), F32)

    def put(kind, y, place, first, second):
        rows = pl.ds(place * 64, 64)
        w_v[y, kind, rows, 0:128] = first.astype(BF16)
        w_v[y, kind, rows, 128:256] = second.astype(BF16)

    for y in range(4):
        for side in range(2):
            inv = inv_v[side, y].astype(F32)
            for z in range(2):
                place = 2 * side + z
                block = jnp.where(low if z == 0 else jnp.logical_not(low), inv, 0.0)
                tiles = [block, zero] if side == 0 else [zero, block]
                wb_v[y, pl.ds(place * 64, 64), 0:128] = tiles[0].astype(BF16)
                wb_v[y, pl.ds(place * 64, 64), 128:256] = tiles[1].astype(BF16)

                a = sten_v[side, y, z, :, 0:128].astype(F32)
                b = sten_v[side, y, z, :, 128:256].astype(F32)
                c = sten_v[side, y, z, :, 256:384].astype(F32)
                d = sten_v[side, y, z, :, 384:448].astype(F32)
                d = jnp.concatenate([d, d], axis=1)
                ra, rb, rc = swap(a), swap(b), swap(c)
                if z == 0:
                    own = jnp.where(low, a, d)
                    toward_o, toward_i = jnp.where(is_odd, b, ra), jnp.where(is_odd, ra, b)
                    toward_m, toward_p = rb, c
                    keep = low
                else:
                    own = jnp.where(low, rc, ra)
                    toward_o, toward_i = jnp.where(is_odd, rb, a), jnp.where(is_odd, a, rb)
                    toward_m, toward_p = b, rc
                    keep = jnp.logical_not(low)
                toward_o = jnp.where(keep, toward_o, 0.0)
                toward_i = jnp.where(keep, toward_i, 0.0)
                toward_m = jnp.where(keep, toward_m, 0.0)
                toward_p = jnp.where(keep, toward_p, 0.0)
                if y == 0:
                    toward_m = jnp.where(has_below, toward_m, 0.0)
                if y == 3:
                    toward_p = jnp.where(has_above, toward_p, 0.0)
                if side == 0:
                    put(0, y, place, own, toward_i)
                    put(1, y, place, jnp.where(has_outer, toward_o, 0.0), zero)
                    put(2, y, place, toward_m, zero)
                    put(3, y, place, toward_p, zero)
                else:
                    put(0, y, place, toward_o, own)
                    put(1, y, place, zero, toward_i)
                    put(2, y, place, zero, toward_m)
                    put(3, y, place, zero, toward_p)

    def first_slot(y):
        applied = nt(st_v[y], w_v[y, 0])
        if y > 0:
            applied = applied + nt(st_v[y - 1], w_v[y, 2])
        if y < 3:
            applied = applied + nt(st_v[y + 1], w_v[y, 3])
        relaxed = nt(applied.astype(BF16), wb_v[y])
        p0_v[y] = (st_v[y].astype(F32) - RELAX * relaxed).astype(BF16)

    first_slot(0)
    first_y = [send(p0_v.at[0], hp0y_v.at[1], (gx, below))]
    first_slot(3)
    first_y.append(send(p0_v.at[3], hp0y_v.at[0], (gx, above)))
    first_slot(1)
    first_slot(2)
    first_x = [
        send(p0_v.at[:, :, 0:128], hp0x_v.at[:, :, 0:128], (outer, gy)),
        send(p0_v.at[:, :, 128:256], hp0x_v.at[:, :, 128:256], (partner, gy)),
    ]

    for copy in seed_x + seed_y:
        copy.wait_recv()

    def side_slots(y):
        halo = jnp.concatenate([hx_v[0, y], hx_v[1, y]], axis=1)
        halos, applied = [halo], [nt(halo, w_v[y, 1]).astype(BF16)]
        if y in (0, 3):
            end = 0 if y == 0 else 1
            halo = jnp.concatenate([hy_v[end, 0], hy_v[end, 1]], axis=1)
            halos.append(halo)
            applied.append(nt(halo, w_v[y, 2 + end]).astype(BF16))
        applied = applied[0] if len(applied) == 1 else jnp.concatenate(applied, axis=0)
        relaxed = nt(applied, wb_v[y])
        for n, at in enumerate([X_AT[y]] + ([Y_AT[y]] if y in Y_AT else [])):
            values = -RELAX * relaxed[16 * n : 16 * n + MODES]
            tile = jnp.concatenate([values, halos[n][MODES:].astype(F32)], axis=0)
            pc_v[at] = tile.astype(BF16)

    side_slots(0)
    side_slots(3)
    side_y = [
        send(pc_v.at[0:2], hpcy_v.at[1], (gx, below)),
        send(pc_v.at[4:6], hpcy_v.at[0], (gx, above)),
    ]
    side_slots(1)
    side_slots(2)
    side_x = [
        send(pc_v.at[:, :, 0:128], hpcx_v.at[:, :, 0:128], (outer, gy)),
        send(pc_v.at[:, :, 128:256], hpcx_v.at[:, :, 128:256], (partner, gy)),
    ]

    out[...] = jnp.zeros(out.shape, F32)
    blank = jnp.zeros((64, 128), BF16)
    for y in range(4):
        full = expand(pc_v[X_AT[y]])
        lx_v[y, 0:64, 0:128] = full[:, 0:128]
        lx_v[y, 0:64, 128:256] = blank
        lx_v[y, 64:128, 0:128] = blank
        lx_v[y, 64:128, 128:256] = full[:, 128:256]
        if y in Y_AT:
            lx_v[y, 128:192] = expand(pc_v[Y_AT[y]])

    def left(y, rows):
        return jnp.concatenate([p0_v[y], lx_v[y, 0 : rows - 64]], axis=0)

    terms = [jnp.zeros((64, 1), F32) for slot in range(5)]
    for y in range(4):
        res = jnp.concatenate([res_v[0, y : y + 1, :], res_v[1, y : y + 1, :]], axis=1)
        blocks = [(0, p0_v[y]), (1, lx_v[y, 0:64]), (2, lx_v[y, 64:128])]
        if y in Y_AT:
            blocks.append((3 if y == 0 else 4, lx_v[y, 128:192]))
        for slot, block in blocks:
            terms[slot] = terms[slot] + jnp.sum(block.astype(F32) * res, axis=1, keepdims=True)

    for y in range(4):
        size = 256 if y in Y_AT else 192
        acc_v[y, 0:size] = nt(left(y, size), w_v[y, 0])
        if y not in Y_AT:
            acc_v[y, 192:256] = jnp.zeros((64, 256), F32)
        if y > 0:
            size = 256 if y - 1 in Y_AT else 192
            acc_v[y, 0:size] = acc_v[y, 0:size] + nt(left(y - 1, size), w_v[y, 2])
        if y < 3:
            size = 256 if y + 1 in Y_AT else 192
            acc_v[y, 0:size] = acc_v[y, 0:size] + nt(left(y + 1, size), w_v[y, 3])

    for copy in first_x + first_y:
        copy.wait_recv()
    for y in range(4):
        part = nt(hp0x_v[y], w_v[y, 1])
        acc_v[y, 64:128, 0:128] = acc_v[y, 64:128, 0:128] + part[:, 0:128]
        acc_v[y, 128:192, 128:256] = acc_v[y, 128:192, 128:256] + part[:, 128:256]
        if y in Y_AT:
            end = 0 if y == 0 else 1
            acc_v[y, 192:256] = acc_v[y, 192:256] + nt(hp0y_v[end], w_v[y, 2 + end])

    for copy in side_y + side_x:
        copy.wait_recv()

    def finish(y):
        if y in Y_AT:
            end = 0 if y == 0 else 1
            fromx = jnp.concatenate([expand(hpcx_v[X_AT[y]]), expand(hpcx_v[Y_AT[y]])], axis=0)
            partx = nt(fromx, w_v[y, 1])
            fromy = jnp.concatenate([expand(hpcy_v[end, 0]), expand(hpcy_v[end, 1])], axis=0)
            party = nt(fromy, w_v[y, 2 + end])
            own = (acc_v[y, 0:64] + partx[0:64] + party[64:128]).astype(BF16)
            corner = (partx[64:128] + party[0:64]).astype(BF16)
            mid = acc_v[y, 64:256].astype(BF16)
            corner_o = jnp.concatenate([corner[:, 0:128], blank], axis=1)
            corner_i = jnp.concatenate([blank, corner[:, 128:256]], axis=1)
            right = jnp.concatenate(
                [own, mid[128:192], corner_o, mid[0:64], corner_i, mid[64:128]], axis=0
            )
            return nt(left(y, 256), right)
        partx = nt(expand(hpcx_v[X_AT[y]]), w_v[y, 1])
        own = (acc_v[y, 0:64] + partx).astype(BF16)
        mid = acc_v[y, 64:256].astype(BF16)
        right = jnp.concatenate([own, mid[128:192], mid[64:128], mid[0:64]], axis=0)
        return nt(left(y, 192), right)

    def pick(first, second):
        return jnp.where(low, first, second)

    def half(tile, near):
        moved = jnp.where(low, tile, pltpu.roll(tile, 96, 1))
        return jnp.where(is_odd, moved, tile) if near else jnp.where(is_odd, tile, moved)

    def with_terms(tile, term):
        upper = term.astype(BF16).astype(F32)
        return jnp.where(wide == 96, upper, jnp.where(wide == 97, term - upper, tile))

    def tiles(product, slot):
        rows = product[slot * 64 : slot * 64 + 64]
        return [rows[:, 128 * t : 128 * t + 128] for t in range(rows.shape[1] // 128)]

    def post(at, values):
        for n, value in enumerate(values):
            snd_v[at + n] = value.astype(BF16)

    g0 = finish(0)
    t0, t1, t2 = tiles(g0, 3)
    post(8, [with_terms(half(pick(jnp.where(is_odd, t0, 0.0), t0), True), terms[3]), t1])
    post(10, [half(pick(jnp.where(is_odd, 0.0, t0), t0), False), t2])
    msgs = [
        send(snd_v.at[8:10], rcv_v.at[8:10], (gx, below)),
        send(snd_v.at[10:12], rcv_v.at[10:12], (partner, below)),
    ]
    g3 = finish(3)
    t0, t1, t2 = tiles(g3, 3)
    post(12, [with_terms(half(pick(jnp.where(is_odd, 0.0, t0), t0), True), terms[4]), t1])
    post(14, [half(pick(jnp.where(is_odd, t0, 0.0), t0), False), t2])
    msgs += [
        send(snd_v.at[12:14], rcv_v.at[12:14], (gx, above)),
        send(snd_v.at[14:16], rcv_v.at[14:16], (partner, above)),
    ]
    g1 = finish(1)
    g2 = finish(2)

    def summed(slot):
        a0, a1, a2 = tiles(g0, slot)
        b0, b1, b2 = tiles(g3, slot)
        c0, c1 = tiles(g1, slot)
        d0, d1 = tiles(g2, slot)
        um, up = a0 + c0, b0 + d0
        mid = c1 + d1
        return um, up, um + up, a1, b1, a1 + b1 + mid, a2, b2, a2 + b2 + swap(mid)

    def by_side(first, second):
        return jnp.where(is_odd, second, first)

    um, up, mid, om, op, o_sum, im, ip, i_sum = summed(1)
    post(
        4,
        [
            with_terms(half(pick(by_side(op, om), o_sum), False), terms[1]),
            pick(mid, up),
            pick(swap(um), i_sum),
        ],
    )
    post(7, [half(pick(by_side(om, op), o_sum), True)])
    msgs += [
        send(snd_v.at[4:7], rcv_v.at[4:7], (outer, gy)),
        send(snd_v.at[7:8], rcv_v.at[7:8], (outer2, gy)),
    ]
    um, up, mid, om, op, o_sum, im, ip, i_sum = summed(2)
    post(3, [with_terms(half(pick(by_side(ip, im), i_sum), False), terms[2])])
    far_a = half(pick(by_side(im, ip), i_sum), True)
    far_b = pick(mid, up)
    far_c = pick(swap(um), o_sum)
    um, up, mid, om, op, o_sum, im, ip, i_sum = summed(0)
    post(
        0,
        [
            half(swap(pick(mid, by_side(up, um))), False),
            swap(pick(ip, i_sum)),
            pick(im, 0.0),
        ],
    )
    msgs += [send(snd_v.at[0:4], rcv_v.at[0:4], (partner, gy))]
    own_a = with_terms(half(swap(pick(mid, by_side(um, up))), True), terms[0])
    own_b = swap(pick(op, o_sum))
    own_c = pick(om, 0.0)

    for copy in msgs:
        copy.wait_recv()

    def got(at):
        return rcv_v[at].astype(F32)

    y_near, y_far = got(13), got(15)
    own_a = own_a + got(3) + got(4) + got(8) + got(12)
    own_b = own_b + got(5) + got(9) + pick(y_near, 0.0)
    own_c = own_c + got(6) + pick(swap(y_near), 0.0)
    far_a = far_a + got(0) + got(7) + got(10) + got(14)
    far_b = far_b + got(1) + got(11) + pick(y_far, 0.0)
    far_c = far_c + got(2) + pick(swap(y_far), 0.0)

    def both(own, far):
        first, second = jnp.where(is_odd, far, own), jnp.where(is_odd, own, far)
        return jnp.concatenate([first, second], axis=0).T

    a, b, c = both(own_a, far_a), both(own_b, far_b), both(own_c, far_c)

    @pl.when(odd == 0)
    def _():
        out[128:192] = c[64:128]
        out[320:384] = c[0:64]
        out[384:512] = b
        out[704:800] = a[0:96]
        out[800:801] = a[96:97] + a[97:98]

    @pl.when(odd == 1)
    def _():
        out[0:32] = a[64:96]
        out[32:96] = a[0:64]
        out[288:352] = c[0:64]
        out[352:480] = b
        out[608:672] = c[64:128]
        out[800:801] = swap(a[96:97] + a[97:98])

    for copy in sends:
        copy.wait_send()


def finish_kernel(data, coarse, restricted, row, sem):
    first = pltpu.make_async_copy(data.at[pl.ds(0, 800)], coarse.at[0, 0], sem.at[0])
    first.start()
    row[...] = data[800:801, 0:64]
    second = pltpu.make_async_copy(row, restricted.at[0], sem.at[1])
    second.start()
    first.wait()
    second.wait()


def body(stencil, inverse, tentative, aggregate, residual):
    hbm = pl.BlockSpec(memory_space=pltpu.HBM)
    aggregate = aggregate.transpose(0, 2, 1)
    operands = [
        pltpu.with_memory_space_constraint(operand, pltpu.HBM)
        for operand in (stencil, inverse, tentative, aggregate, residual)
    ]
    vmem = pl.BlockSpec(memory_space=pltpu.VMEM)
    scratch = [
        pltpu.VMEM(stencil.shape, BF16),
        pltpu.VMEM(inverse.shape, BF16),
        pltpu.VMEM(tentative.shape, BF16),
        pltpu.VMEM(aggregate.shape, jnp.int32),
        pltpu.VMEM(residual.shape, F32),
        pltpu.VMEM((4, 4, 256, 256), BF16),
        pltpu.VMEM((4, 256, 256), BF16),
        pltpu.VMEM((2, 4, 16, 128), BF16),
        pltpu.VMEM((2, 4, 16, 128), BF16),
        pltpu.VMEM((2, 2, 16, 128), BF16),
        pltpu.VMEM((4, 64, 256), BF16),
        pltpu.VMEM((4, 64, 256), BF16),
        pltpu.VMEM((2, 64, 256), BF16),
        pltpu.VMEM((6, 16, 256), BF16),
        pltpu.VMEM((6, 16, 256), BF16),
        pltpu.VMEM((2, 2, 16, 256), BF16),
        pltpu.VMEM((4, 64, 256), BF16),
        pltpu.VMEM((4, 192, 256), BF16),
        pltpu.VMEM((4, 256, 256), F32),
        pltpu.VMEM((16, 64, 128), BF16),
        pltpu.VMEM((16, 64, 128), BF16),
        pltpu.SemaphoreType.DMA((10,)),
        pltpu.SemaphoreType.DMA((19,)),
        pltpu.SemaphoreType.DMA((19,)),
    ]
    sizes = (lax.axis_size("gx"), lax.axis_size("gy"))

    def call(*refs):
        kernel(*sizes, *refs)

    coarse = pl.pallas_call(
        call,
        out_shape=pltpu.VMEM((808, 128), F32),
        in_specs=[hbm] * 5,
        out_specs=vmem,
        scratch_shapes=scratch,
        compiler_params=pltpu.CompilerParams(
            collective_id=0, has_side_effects=True, vmem_limit_bytes=32 << 20
        ),
        name="galerkin",
    )(*operands)
    coarse, restricted = pl.pallas_call(
        finish_kernel,
        out_shape=(
            jax.ShapeDtypeStruct((1, 1, 800, 128), F32),
            jax.ShapeDtypeStruct((1, 1, 64), F32),
        ),
        in_specs=[pl.BlockSpec(memory_space=pltpu.VMEM)],
        out_specs=(pl.BlockSpec(memory_space=pl.ANY), pl.BlockSpec(memory_space=pl.ANY)),
        scratch_shapes=[pltpu.VMEM((1, 64), F32), pltpu.SemaphoreType.DMA((2,))],
        name="store",
    )(pltpu.with_memory_space_constraint(coarse, pltpu.VMEM))
    return coarse.swapaxes(2, 3), restricted


def solution(mesh):
    in_specs = (
        P("gx", "gy", None, None, None),
        P("gx", "gy", None, None),
        P("gx", "gy", None, None),
        P("gx", "gy", None),
        P("gx", "gy", None),
    )
    out_specs = (P("gx", "gy", None, None), P("gx", "gy", None))
    return jax.shard_map(body, mesh=mesh, in_specs=in_specs, out_specs=out_specs, check_vma=False)
```

```python
import jax
import jax.numpy as jnp
from jax import lax
from jax.experimental import pallas as pl
from jax.experimental.pallas import tpu as pltpu
from jax.sharding import PartitionSpec as P

MESH = pl.DeviceIdType.MESH
F32, BF16 = jnp.float32, jnp.bfloat16
AGG = 8
MODES = 8
RELAX = 0.6


X_AT, Y_AT = (0, 2, 3, 4), {0: 1, 3: 5}


def nt(left, right):
    return lax.dot_general(left, right, (((1,), (1,)), ((), ())), preferred_element_type=F32)


def expand(tile):
    values, code = tile[0:MODES].astype(F32), tile[MODES : 2 * MODES].astype(F32)
    rows = [jnp.where(code == float(a), values, 0.0) for a in range(AGG)]
    return jnp.concatenate(rows, axis=0).astype(BF16)


def swap(tile):
    return pltpu.roll(tile, 64, 1)


def kernel(
    n_gx,
    n_gy,
    stencil,
    inverse,
    tentative,
    aggregate,
    residual,
    out,
    sten_v,
    inv_v,
    tent_v,
    agg_v,
    res_v,
    w_v,
    wb_v,
    hxt_v,
    hxa_v,
    hyt_v,
    hya_v,
    p0_v,
    hp0x_v,
    hp0y_v,
    pc_v,
    hpcx_v,
    hpcy_v,
    st_v,
    lx_v,
    acc_v,
    snd_v,
    rcv_v,
    sny_v,
    rcy_v,
    load_sem,
    send_sem,
    recv_sem,
):
    gx, gy = lax.axis_index("gx"), lax.axis_index("gy")
    odd = lax.rem(gx, 2)
    is_odd = odd == 1
    turn = 2 * odd - 1
    partner = gx - turn
    outer = lax.rem(gx + turn + n_gx, n_gx)
    outer2 = lax.rem(gx + 2 * turn + n_gx, n_gx)
    back2 = lax.rem(gx - 2 * turn + n_gx, n_gx)
    below = lax.rem(gy - 1 + n_gy, n_gy)
    above = lax.rem(gy + 1, n_gy)
    has_outer = jnp.logical_and(gx > 0, gx < n_gx - 1)
    has_back = jnp.logical_and(partner > 0, partner < n_gx - 1)
    has_below, has_above = gy > 0, gy < n_gy - 1

    def only(condition, action):
        if condition is None:
            action()
        else:
            pl.when(condition)(action)

    barrier = pltpu.get_barrier_semaphore()
    peers = [
        ((gx, above), has_above),
        ((partner, above), has_above),
        ((gx, below), has_below),
        ((partner, below), has_below),
        ((outer, gy), has_outer),
        ((outer2, gy), has_outer),
        ((back2, gy), has_back),
        ((partner, gy), None),
    ]
    for peer, condition in peers:
        only(
            condition,
            lambda peer=peer: pl.semaphore_signal(
                barrier, inc=1, device_id=peer, device_id_type=MESH
            ),
        )
    awaited = 1
    for _, condition in peers[:-1]:
        awaited = awaited + jnp.where(condition, 1, 0)

    loads = []

    def load(src, dst):
        copy = pltpu.make_async_copy(src, dst, load_sem.at[len(loads)])
        copy.start()
        loads.append(copy)
        return copy

    small = []
    for side in range(2):
        x = side + odd - 2 * side * odd
        small.append(load(tentative.at[x], tent_v.at[side]))
        small.append(load(aggregate.at[x], agg_v.at[side]))
    big = []
    for side in range(2):
        x = side + odd - 2 * side * odd
        big.append(load(stencil.at[x], sten_v.at[side]))
        big.append(load(inverse.at[x], inv_v.at[side]))
        big.append(load(residual.at[x], res_v.at[side]))

    sends = []

    def send(src, dst, peer, leaves=None, arrives=None):
        at = len(sends)
        copy = pltpu.make_async_remote_copy(
            src_ref=src,
            dst_ref=dst,
            send_sem=send_sem.at[at],
            recv_sem=recv_sem.at[at],
            device_id=peer,
            device_id_type=MESH,
        )
        only(leaves, copy.start)
        sends.append((copy, leaves))
        return copy, arrives

    def await_all(copies):
        for copy, arrives in copies:
            only(arrives, copy.wait_recv)

    to_outer, to_outer2 = (has_outer, has_outer), (has_outer, has_back)
    to_below, to_above = (has_below, has_above), (has_above, has_below)

    pl.semaphore_wait(barrier, awaited)
    x_of = [odd, 1 - odd]
    seeds = [
        send(tentative.at[:, 3], hyt_v.at[0], (gx, above), *to_above),
        send(aggregate, hya_v.at[0], (gx, above), *to_above),
        send(tentative.at[:, 0], hyt_v.at[1], (gx, below), *to_below),
        send(aggregate, hya_v.at[1], (gx, below), *to_below),
        send(tentative.at[x_of[0]], hxt_v.at[0], (outer, gy), *to_outer),
        send(aggregate.at[x_of[0]], hxa_v.at[0], (outer, gy), *to_outer),
        send(tentative.at[x_of[1]], hxt_v.at[1], (partner, gy)),
        send(aggregate.at[x_of[1]], hxa_v.at[1], (partner, gy)),
    ]

    @pl.when(jnp.logical_not(has_outer))
    def _():
        hxt_v[0] = jnp.zeros(hxt_v.shape[1:], BF16)
        hxa_v[0] = jnp.zeros(hxa_v.shape[1:], jnp.int32)
        hp0x_v[:, :, 0:128] = jnp.zeros((4, 64, 128), BF16)
        hpcx_v[:, :, 0:128] = jnp.zeros((6, 16, 128), BF16)
        rcv_v[4:7] = jnp.zeros((3, 64, 128), BF16)

    @pl.when(jnp.logical_not(has_back))
    def _():
        rcv_v[7] = jnp.zeros((64, 128), BF16)

    for end, condition in enumerate((has_below, has_above)):

        @pl.when(jnp.logical_not(condition))
        def _(end=end):
            hyt_v[end] = jnp.zeros(hyt_v.shape[1:], BF16)
            hya_v[end] = jnp.zeros(hya_v.shape[1:], jnp.int32)
            hp0y_v[end] = jnp.zeros((64, 256), BF16)
            hpcy_v[end] = jnp.zeros((2, 16, 256), BF16)
            rcy_v[end] = jnp.zeros((4, 32, 128), BF16)

    lane = lax.broadcasted_iota(jnp.int32, (8, 128), 1)
    def packed(modes, code_0, code_1):
        code = jnp.where(
            lane < 64, jnp.broadcast_to(code_0, (8, 128)), jnp.broadcast_to(code_1, (8, 128))
        )
        return jnp.concatenate([modes.astype(F32), code.astype(F32)], axis=0).astype(BF16)

    for copy in small:
        copy.wait()

    for y in range(4):
        row = pl.ds(y, 1)
        tiles = [
            packed(tent_v[side, y], agg_v[side, 0:1, row], agg_v[side, 1:2, row])
            for side in range(2)
        ]
        st_v[y] = expand(jnp.concatenate(tiles, axis=1))

    for copy in big:
        copy.wait()
    wide = lax.broadcasted_iota(jnp.int32, (64, 128), 1)
    low = wide < 64
    zero = jnp.zeros((64, 128), F32)

    def put(kind, y, place, first, second):
        rows = pl.ds(place * 64, 64)
        w_v[y, kind, rows, 0:128] = first.astype(BF16)
        w_v[y, kind, rows, 128:256] = second.astype(BF16)

    for y in range(4):
        for side in range(2):
            inv = inv_v[side, y].astype(F32)
            for z in range(2):
                place = 2 * side + z
                block = jnp.where(low if z == 0 else jnp.logical_not(low), inv, 0.0)
                tiles = [block, zero] if side == 0 else [zero, block]
                wb_v[y, pl.ds(place * 64, 64), 0:128] = tiles[0].astype(BF16)
                wb_v[y, pl.ds(place * 64, 64), 128:256] = tiles[1].astype(BF16)

                a = sten_v[side, y, z, :, 0:128].astype(F32)
                b = sten_v[side, y, z, :, 128:256].astype(F32)
                c = sten_v[side, y, z, :, 256:384].astype(F32)
                d = sten_v[side, y, z, :, 384:448].astype(F32)
                d = jnp.concatenate([d, d], axis=1)
                ra, rb, rc = swap(a), swap(b), swap(c)
                if z == 0:
                    own = jnp.where(low, a, d)
                    toward_o, toward_i = jnp.where(is_odd, b, ra), jnp.where(is_odd, ra, b)
                    toward_m, toward_p = rb, c
                    keep = low
                else:
                    own = jnp.where(low, rc, ra)
                    toward_o, toward_i = jnp.where(is_odd, rb, a), jnp.where(is_odd, a, rb)
                    toward_m, toward_p = b, rc
                    keep = jnp.logical_not(low)
                toward_o = jnp.where(keep, toward_o, 0.0)
                toward_i = jnp.where(keep, toward_i, 0.0)
                toward_m = jnp.where(keep, toward_m, 0.0)
                toward_p = jnp.where(keep, toward_p, 0.0)
                if side == 0:
                    put(0, y, place, own, toward_i)
                    put(1, y, place, toward_o, zero)
                    put(2, y, place, toward_m, zero)
                    put(3, y, place, toward_p, zero)
                else:
                    put(0, y, place, toward_o, own)
                    put(1, y, place, zero, toward_i)
                    put(2, y, place, zero, toward_m)
                    put(3, y, place, zero, toward_p)

    applied = {}
    for y in (3, 0, 1, 2):
        total = nt(st_v[y], w_v[y, 0])
        if y > 0:
            total = total + nt(st_v[y - 1], w_v[y, 2])
        if y < 3:
            total = total + nt(st_v[y + 1], w_v[y, 3])
        applied[y] = total.astype(BF16)
    for y in (3, 0, 1, 2):
        relaxed = nt(applied[y], wb_v[y])
        p0_v[y] = (st_v[y].astype(F32) - RELAX * relaxed).astype(BF16)
    first = [
        send(p0_v.at[3], hp0y_v.at[0], (gx, above), *to_above),
        send(p0_v.at[0], hp0y_v.at[1], (gx, below), *to_below),
        send(p0_v.at[:, :, 0:128], hp0x_v.at[:, :, 0:128], (outer, gy), *to_outer),
        send(p0_v.at[:, :, 128:256], hp0x_v.at[:, :, 128:256], (partner, gy)),
    ]

    await_all(seeds)
    halos, codes = {}, {}
    for end, y in ((1, 3), (0, 0)):
        row = pl.ds(3 - y, 1)
        cells = [
            [hya_v[end, x_of[side], z : z + 1, row] for z in range(2)] for side in range(2)
        ]
        codes[y] = cells[0] + cells[1]
        tiles = [packed(hyt_v[end, x_of[side]], *cells[side]) for side in range(2)]
        halos[Y_AT[y]] = jnp.concatenate(tiles, axis=1)
    for y in (3, 0, 1, 2):
        row = pl.ds(y, 1)
        tiles = [
            packed(hxt_v[side, y], hxa_v[side, 0:1, row], hxa_v[side, 1:2, row])
            for side in range(2)
        ]
        halos[X_AT[y]] = jnp.concatenate(tiles, axis=1)
    applied = {}
    for y in (3, 0, 1, 2):
        applied[y] = nt(halos[X_AT[y]], w_v[y, 1]).astype(BF16)
        if y in Y_AT:
            more = nt(halos[Y_AT[y]], w_v[y, 2 if y == 0 else 3]).astype(BF16)
            applied[y] = jnp.concatenate([applied[y], more], axis=0)
    for y in (3, 0, 1, 2):
        relaxed = nt(applied[y], wb_v[y])
        for n, at in enumerate([X_AT[y]] + ([Y_AT[y]] if y in Y_AT else [])):
            values = -RELAX * relaxed[16 * n : 16 * n + MODES]
            tile = jnp.concatenate([values, halos[at][MODES:].astype(F32)], axis=0)
            pc_v[at] = tile.astype(BF16)
    side = [
        send(pc_v.at[4:6], hpcy_v.at[0], (gx, above), *to_above),
        send(pc_v.at[0:2], hpcy_v.at[1], (gx, below), *to_below),
        send(pc_v.at[:, :, 0:128], hpcx_v.at[:, :, 0:128], (outer, gy), *to_outer),
        send(pc_v.at[:, :, 128:256], hpcx_v.at[:, :, 128:256], (partner, gy)),
    ]

    out[...] = jnp.zeros(out.shape, F32)
    blank = jnp.zeros((64, 128), BF16)
    for y in range(4):
        full = expand(pc_v[X_AT[y]])
        lx_v[y, 0:64, 0:128] = full[:, 0:128]
        lx_v[y, 0:64, 128:256] = blank
        lx_v[y, 64:128, 0:128] = blank
        lx_v[y, 64:128, 128:256] = full[:, 128:256]
        if y in Y_AT:
            lx_v[y, 128:192] = expand(pc_v[Y_AT[y]])

    def left(y, rows):
        return jnp.concatenate([p0_v[y], lx_v[y, 0 : rows - 64]], axis=0)

    lane_wide = lax.broadcasted_iota(jnp.int32, (MODES, 256), 1)
    ly = {}
    for y in Y_AT:
        values = pc_v[Y_AT[y]][0:MODES].astype(F32)
        parts = [
            jnp.where(jnp.logical_and(lane_wide >= 64 * e, lane_wide < 64 * e + 64), values, 0.0)
            for e in range(4)
        ]
        ly[y] = jnp.concatenate(parts, axis=0).astype(BF16)

    terms = [jnp.zeros((rows, 1), F32) for rows in (64, 64, 64, 32, 32)]
    for y in range(4):
        res = jnp.concatenate([res_v[0, y : y + 1, :], res_v[1, y : y + 1, :]], axis=1)
        blocks = [(0, p0_v[y]), (1, lx_v[y, 0:64]), (2, lx_v[y, 64:128])]
        if y in Y_AT:
            blocks.append((3 if y == 0 else 4, ly[y]))
        for slot, block in blocks:
            terms[slot] = terms[slot] + jnp.sum(block.astype(F32) * res, axis=1, keepdims=True)

    for y in range(4):
        size = 256 if y in Y_AT else 192
        acc_v[y, 0:size] = nt(left(y, size), w_v[y, 0])
        if y not in Y_AT:
            acc_v[y, 192:256] = jnp.zeros((64, 256), F32)
        if y > 0:
            size = 256 if y - 1 in Y_AT else 192
            acc_v[y, 0:size] = acc_v[y, 0:size] + nt(left(y - 1, size), w_v[y, 2])
        if y < 3:
            size = 256 if y + 1 in Y_AT else 192
            acc_v[y, 0:size] = acc_v[y, 0:size] + nt(left(y + 1, size), w_v[y, 3])

    await_all(first)
    for y in range(4):
        part = nt(hp0x_v[y], w_v[y, 1])
        acc_v[y, 64:128, 0:128] = acc_v[y, 64:128, 0:128] + part[:, 0:128]
        acc_v[y, 128:192, 128:256] = acc_v[y, 128:192, 128:256] + part[:, 128:256]
        if y in Y_AT:
            end = 0 if y == 0 else 1
            acc_v[y, 192:256] = acc_v[y, 192:256] + nt(hp0y_v[end], w_v[y, 2 + end])

    await_all(side)

    def finish(y):
        if y in Y_AT:
            end = 0 if y == 0 else 1
            fromx = jnp.concatenate([expand(hpcx_v[X_AT[y]]), expand(hpcx_v[Y_AT[y]])], axis=0)
            partx = nt(fromx, w_v[y, 1])
            fromy = jnp.concatenate([expand(hpcy_v[end, 0]), expand(hpcy_v[end, 1])], axis=0)
            party = nt(fromy, w_v[y, 2 + end])
            own = (acc_v[y, 0:64] + partx[0:64] + party[64:128]).astype(BF16)
            corner = (partx[64:128] + party[0:64]).astype(BF16)
            mid = acc_v[y, 64:256].astype(BF16)
            corner_o = jnp.concatenate([corner[:, 0:128], blank], axis=1)
            corner_i = jnp.concatenate([blank, corner[:, 128:256]], axis=1)
            right = jnp.concatenate(
                [own, mid[128:192], corner_o, mid[0:64], corner_i, mid[64:128]], axis=0
            )
            return nt(jnp.concatenate([left(y, 192), ly[y]], axis=0), right)
        partx = nt(expand(hpcx_v[X_AT[y]]), w_v[y, 1])
        own = (acc_v[y, 0:64] + partx).astype(BF16)
        mid = acc_v[y, 64:256].astype(BF16)
        right = jnp.concatenate([own, mid[128:192], mid[64:128], mid[0:64]], axis=0)
        return nt(left(y, 192), right)

    def pick(first, second):
        shape = first.shape if hasattr(first, "shape") else second.shape
        return jnp.where(wide[0 : shape[0]] < 64, first, second)

    def half(tile, near):
        moved = pick(tile, pltpu.roll(tile, 96, 1))
        return jnp.where(is_odd, moved, tile) if near else jnp.where(is_odd, tile, moved)

    def with_terms(tile, term):
        upper = term.astype(BF16).astype(F32)
        at = wide[0 : tile.shape[0]]
        return jnp.where(at == 96, upper, jnp.where(at == 97, term - upper, tile))

    def with_codes(tile, y):
        column = jnp.concatenate(
            [jnp.broadcast_to(cell, (MODES, 128)) for cell in codes[y]], axis=0
        )
        return jnp.where(wide[0:32] == 112, column.astype(F32), tile)

    def tiles(product, slot):
        rows = product[slot * 64 : slot * 64 + 64]
        return [rows[:, 128 * t : 128 * t + 128] for t in range(rows.shape[1] // 128)]

    def post(at, values):
        for n, value in enumerate(values):
            snd_v[at + n] = value.astype(BF16)

    msgs = []
    g3, g0 = finish(3), finish(0)
    for end, g, y, peer, way in ((1, g3, 3, above, to_above), (0, g0, 0, below, to_below)):
        t0, t1, t2 = [g[192:224, 128 * t : 128 * t + 128] for t in range(3)]
        kept = (jnp.where(is_odd, 0.0, t0), t0) if end else (jnp.where(is_odd, t0, 0.0), t0)
        near = half(pick(*kept), True)
        kept = (jnp.where(is_odd, t0, 0.0), t0) if end else (jnp.where(is_odd, 0.0, t0), t0)
        far = half(pick(*kept), False)
        sny_v[end, 0] = with_codes(with_terms(near, terms[3 + end]), y).astype(BF16)
        sny_v[end, 1] = t1.astype(BF16)
        sny_v[end, 2] = with_codes(far, y).astype(BF16)
        sny_v[end, 3] = t2.astype(BF16)
        msgs += [
            send(sny_v.at[end, 0:2], rcy_v.at[1 - end, 0:2], (gx, peer), *way),
            send(sny_v.at[end, 2:4], rcy_v.at[1 - end, 2:4], (partner, peer), *way),
        ]
    g1 = finish(1)
    g2 = finish(2)

    def summed(slot):
        a0, a1, a2 = tiles(g0, slot)
        b0, b1, b2 = tiles(g3, slot)
        c0, c1 = tiles(g1, slot)
        d0, d1 = tiles(g2, slot)
        um, up = a0 + c0, b0 + d0
        mid = c1 + d1
        return um, up, um + up, a1, b1, a1 + b1 + mid, a2, b2, a2 + b2 + swap(mid)

    def by_side(first, second):
        return jnp.where(is_odd, second, first)

    um, up, mid, om, op, o_sum, im, ip, i_sum = summed(1)
    post(
        4,
        [
            with_terms(half(pick(by_side(op, om), o_sum), False), terms[1]),
            pick(mid, up),
            pick(swap(um), i_sum),
        ],
    )
    post(7, [half(pick(by_side(om, op), o_sum), True)])
    msgs += [
        send(snd_v.at[4:7], rcv_v.at[4:7], (outer, gy), *to_outer),
        send(snd_v.at[7:8], rcv_v.at[7:8], (outer2, gy), *to_outer2),
    ]
    um, up, mid, om, op, o_sum, im, ip, i_sum = summed(2)
    post(3, [with_terms(half(pick(by_side(ip, im), i_sum), False), terms[2])])
    far_a = half(pick(by_side(im, ip), i_sum), True)
    far_b = pick(mid, up)
    far_c = pick(swap(um), o_sum)
    um, up, mid, om, op, o_sum, im, ip, i_sum = summed(0)
    post(
        0,
        [
            half(swap(pick(mid, by_side(up, um))), False),
            swap(pick(ip, i_sum)),
            pick(im, 0.0),
        ],
    )
    msgs += [send(snd_v.at[0:4], rcv_v.at[0:4], (partner, gy))]
    own_a = with_terms(half(swap(pick(mid, by_side(um, up))), True), terms[0])
    own_b = swap(pick(op, o_sum))
    own_c = pick(om, 0.0)

    await_all(msgs)

    def got(at):
        return rcv_v[at].astype(F32)

    def spread(end, at):
        first, second = rcy_v[end, at].astype(F32), rcy_v[end, at + 1].astype(F32)
        code = jnp.broadcast_to(first[:, 112:113], (32, 128))
        results = []
        for tile in (first, second):
            rows = []
            for a in range(AGG):
                here = jnp.where(code == float(a), tile, 0.0)
                rows.append(here[0:8] + here[8:16] + here[16:24] + here[24:32])
            results.append(jnp.concatenate(rows, axis=0))
        return results

    (up_a, up_b), (down_a, down_b) = spread(1, 0), spread(0, 0)
    own_a = own_a + got(3) + got(4) + up_a + down_a
    own_b = own_b + got(5) + up_b + pick(down_b, 0.0)
    own_c = own_c + got(6) + pick(swap(down_b), 0.0)
    (up_a, up_b), (down_a, down_b) = spread(1, 2), spread(0, 2)
    far_a = far_a + got(0) + got(7) + up_a + down_a
    far_b = far_b + got(1) + up_b + pick(down_b, 0.0)
    far_c = far_c + got(2) + pick(swap(down_b), 0.0)

    def both(own, far):
        first, second = jnp.where(is_odd, far, own), jnp.where(is_odd, own, far)
        return jnp.concatenate([first, second], axis=0).T

    a, b, c = both(own_a, far_a), both(own_b, far_b), both(own_c, far_c)

    @pl.when(odd == 0)
    def _():
        out[128:192] = c[64:128]
        out[320:384] = c[0:64]
        out[384:512] = b
        out[704:800] = a[0:96]
        out[800:801] = a[96:97] + a[97:98]

    @pl.when(odd == 1)
    def _():
        out[0:32] = a[64:96]
        out[32:96] = a[0:64]
        out[288:352] = c[0:64]
        out[352:480] = b
        out[608:672] = c[64:128]
        out[800:801] = swap(a[96:97] + a[97:98])

    for copy, leaves in sends:
        only(leaves, copy.wait_send)


def finish_kernel(data, coarse, restricted, row, sem):
    first = pltpu.make_async_copy(data.at[pl.ds(0, 800)], coarse.at[0, 0], sem.at[0])
    first.start()
    row[...] = data[800:801, 0:64]
    second = pltpu.make_async_copy(row, restricted.at[0], sem.at[1])
    second.start()
    first.wait()
    second.wait()


def body(stencil, inverse, tentative, aggregate, residual):
    hbm = pl.BlockSpec(memory_space=pltpu.HBM)
    aggregate = aggregate.transpose(0, 2, 1)
    operands = [
        pltpu.with_memory_space_constraint(operand, pltpu.HBM)
        for operand in (stencil, inverse, tentative, aggregate, residual)
    ]
    vmem = pl.BlockSpec(memory_space=pltpu.VMEM)
    scratch = [
        pltpu.VMEM(stencil.shape, BF16),
        pltpu.VMEM(inverse.shape, BF16),
        pltpu.VMEM(tentative.shape, BF16),
        pltpu.VMEM(aggregate.shape, jnp.int32),
        pltpu.VMEM(residual.shape, F32),
        pltpu.VMEM((4, 4, 256, 256), BF16),
        pltpu.VMEM((4, 256, 256), BF16),
        pltpu.VMEM(tentative.shape, BF16),
        pltpu.VMEM(aggregate.shape, jnp.int32),
        pltpu.VMEM((2, 2, 8, 128), BF16),
        pltpu.VMEM((2,) + aggregate.shape, jnp.int32),
        pltpu.VMEM((4, 64, 256), BF16),
        pltpu.VMEM((4, 64, 256), BF16),
        pltpu.VMEM((2, 64, 256), BF16),
        pltpu.VMEM((6, 16, 256), BF16),
        pltpu.VMEM((6, 16, 256), BF16),
        pltpu.VMEM((2, 2, 16, 256), BF16),
        pltpu.VMEM((4, 64, 256), BF16),
        pltpu.VMEM((4, 192, 256), BF16),
        pltpu.VMEM((4, 256, 256), F32),
        pltpu.VMEM((8, 64, 128), BF16),
        pltpu.VMEM((8, 64, 128), BF16),
        pltpu.VMEM((2, 4, 32, 128), BF16),
        pltpu.VMEM((2, 4, 32, 128), BF16),
        pltpu.SemaphoreType.DMA((10,)),
        pltpu.SemaphoreType.DMA((23,)),
        pltpu.SemaphoreType.DMA((23,)),
    ]
    sizes = (lax.axis_size("gx"), lax.axis_size("gy"))

    def call(*refs):
        kernel(*sizes, *refs)

    coarse = pl.pallas_call(
        call,
        out_shape=pltpu.VMEM((808, 128), F32),
        in_specs=[hbm] * 5,
        out_specs=vmem,
        scratch_shapes=scratch,
        compiler_params=pltpu.CompilerParams(
            collective_id=0, has_side_effects=True, vmem_limit_bytes=32 << 20
        ),
        name="galerkin",
    )(*operands)
    coarse, restricted = pl.pallas_call(
        finish_kernel,
        out_shape=(
            jax.ShapeDtypeStruct((1, 1, 800, 128), F32),
            jax.ShapeDtypeStruct((1, 1, 64), F32),
        ),
        in_specs=[pl.BlockSpec(memory_space=pltpu.VMEM)],
        out_specs=(pl.BlockSpec(memory_space=pl.ANY), pl.BlockSpec(memory_space=pl.ANY)),
        scratch_shapes=[pltpu.VMEM((1, 64), F32), pltpu.SemaphoreType.DMA((2,))],
        name="store",
    )(pltpu.with_memory_space_constraint(coarse, pltpu.VMEM))
    return coarse.swapaxes(2, 3), restricted


def solution(mesh):
    in_specs = (
        P("gx", "gy", None, None, None),
        P("gx", "gy", None, None),
        P("gx", "gy", None, None),
        P("gx", "gy", None),
        P("gx", "gy", None),
    )
    out_specs = (P("gx", "gy", None, None), P("gx", "gy", None))
    return jax.shard_map(body, mesh=mesh, in_specs=in_specs, out_specs=out_specs, check_vma=False)
```

```python
import jax
import jax.numpy as jnp
from jax import lax
from jax.experimental import pallas as pl
from jax.experimental.pallas import tpu as pltpu
from jax.sharding import PartitionSpec as P

MESH = pl.DeviceIdType.MESH
F32, BF16 = jnp.float32, jnp.bfloat16
AGG = 8
MODES = 8
RELAX = 0.6


X_AT, Y_AT = (0, 2, 3, 4), {0: 1, 3: 5}


def nt(left, right):
    return lax.dot_general(left, right, (((1,), (1,)), ((), ())), preferred_element_type=F32)


def nn(left, right):
    return lax.dot_general(left, right, (((1,), (0,)), ((), ())), preferred_element_type=F32)


def spread_columns(values, code):
    rows = [jnp.where(code == float(a), values, 0.0) for a in range(AGG)]
    return jnp.concatenate(rows, axis=0).astype(BF16)


def expand(tile):
    return spread_columns(tile[0:MODES].astype(F32), tile[MODES : 2 * MODES].astype(F32))


def by_element(values):
    lane = lax.broadcasted_iota(jnp.int32, (MODES, 256), 1)
    parts = [
        jnp.where(jnp.logical_and(lane >= 64 * e, lane < 64 * e + 64), values, 0.0)
        for e in range(4)
    ]
    return jnp.concatenate(parts, axis=0).astype(BF16)


def far_slot(seed, code, product):
    rows = -RELAX * nt(by_element(seed), product)
    parts = [rows[8 * e : 8 * e + 8] for e in range(4)]
    return spread_columns(jnp.concatenate(parts, axis=1), code)


def swap(tile):
    return pltpu.roll(tile, 64, 1)


def kernel(
    n_gx,
    n_gy,
    stencil,
    inverse,
    tentative,
    aggregate,
    residual,
    out,
    sten_v,
    inv_v,
    tent_v,
    agg_v,
    res_v,
    w_v,
    wb_v,
    pack_v,
    hx_v,
    hy_v,
    hd_v,
    k_v,
    hkx_v,
    hky_v,
    p0_v,
    hp0x_v,
    hp0y_v,
    pc_v,
    corner_v,
    st_v,
    lx_v,
    acc_v,
    snd_v,
    rcv_v,
    sny_v,
    rcy_v,
    load_sem,
    send_sem,
    recv_sem,
):
    gx, gy = lax.axis_index("gx"), lax.axis_index("gy")
    odd = lax.rem(gx, 2)
    is_odd = odd == 1
    turn = 2 * odd - 1
    partner = gx - turn
    outer = lax.rem(gx + turn + n_gx, n_gx)
    outer2 = lax.rem(gx + 2 * turn + n_gx, n_gx)
    back2 = lax.rem(gx - 2 * turn + n_gx, n_gx)
    below = lax.rem(gy - 1 + n_gy, n_gy)
    above = lax.rem(gy + 1, n_gy)
    has_outer = jnp.logical_and(gx > 0, gx < n_gx - 1)
    has_back = jnp.logical_and(partner > 0, partner < n_gx - 1)
    has_below, has_above = gy > 0, gy < n_gy - 1

    def only(condition, action):
        if condition is None:
            action()
        else:
            pl.when(condition)(action)

    barrier = pltpu.get_barrier_semaphore()
    peers = [
        ((gx, above), has_above),
        ((partner, above), has_above),
        ((outer, above), jnp.logical_and(has_outer, has_above)),
        ((gx, below), has_below),
        ((partner, below), has_below),
        ((outer, below), jnp.logical_and(has_outer, has_below)),
        ((outer, gy), has_outer),
        ((outer2, gy), has_outer),
        ((back2, gy), has_back),
        ((partner, gy), None),
    ]
    for peer, condition in peers:
        only(
            condition,
            lambda peer=peer: pl.semaphore_signal(
                barrier, inc=1, device_id=peer, device_id_type=MESH
            ),
        )
    awaited = 1
    for _, condition in peers[:-1]:
        awaited = awaited + jnp.where(condition, 1, 0)

    loads = []

    def load(src, dst):
        copy = pltpu.make_async_copy(src, dst, load_sem.at[len(loads)])
        copy.start()
        loads.append(copy)
        return copy

    small = []
    for side in range(2):
        x = side + odd - 2 * side * odd
        small.append(load(tentative.at[x], tent_v.at[side]))
        small.append(load(aggregate.at[x], agg_v.at[side]))
    big = []
    for side in range(2):
        x = side + odd - 2 * side * odd
        big.append(load(stencil.at[x], sten_v.at[side]))
        big.append(load(inverse.at[x], inv_v.at[side]))
        big.append(load(residual.at[x], res_v.at[side]))

    sends = []

    def send(src, dst, peer, leaves=None, arrives=None):
        at = len(sends)
        copy = pltpu.make_async_remote_copy(
            src_ref=src,
            dst_ref=dst,
            send_sem=send_sem.at[at],
            recv_sem=recv_sem.at[at],
            device_id=peer,
            device_id_type=MESH,
        )
        only(leaves, copy.start)
        sends.append((copy, leaves))
        return copy, arrives

    def await_all(copies):
        for copy, arrives in copies:
            only(arrives, copy.wait_recv)

    to_outer, to_outer2 = (has_outer, has_outer), (has_outer, has_back)
    to_below, to_above = (has_below, has_above), (has_above, has_below)

    @pl.when(jnp.logical_not(has_outer))
    def _():
        hx_v[0] = jnp.zeros(hx_v.shape[1:], BF16)
        hd_v[:, 0] = jnp.zeros((2, 16, 128), BF16)
        hkx_v[:, :, 0:128] = jnp.zeros((6, 64, 128), BF16)
        hp0x_v[:, :, 0:128] = jnp.zeros((4, 64, 128), BF16)
        rcv_v[4:7] = jnp.zeros((3, 64, 128), BF16)

    @pl.when(jnp.logical_not(has_back))
    def _():
        rcv_v[7] = jnp.zeros((64, 128), BF16)

    for end, condition in enumerate((has_below, has_above)):

        @pl.when(jnp.logical_not(condition))
        def _(end=end):
            hy_v[end] = jnp.zeros((2, 16, 128), BF16)
            hd_v[end] = jnp.zeros((2, 16, 128), BF16)
            hky_v[end] = jnp.zeros((2, 64, 256), BF16)
            hp0y_v[end] = jnp.zeros((64, 256), BF16)
            rcy_v[end] = jnp.zeros((4, 32, 128), BF16)

    lane = lax.broadcasted_iota(jnp.int32, (8, 128), 1)
    def packed(modes, code_0, code_1):
        code = jnp.where(
            lane < 64, jnp.broadcast_to(code_0, (8, 128)), jnp.broadcast_to(code_1, (8, 128))
        )
        return jnp.concatenate([modes.astype(F32), code.astype(F32)], axis=0).astype(BF16)

    for copy in small:
        copy.wait()

    own = {}
    for y in range(4):
        row = pl.ds(y, 1)
        tiles = []
        for side in range(2):
            tile = packed(tent_v[side, y], agg_v[side, 0:1, row], agg_v[side, 1:2, row])
            pack_v[side, y] = tile
            tiles.append(tile)
        own[y] = jnp.concatenate(tiles, axis=1).astype(F32)
        st_v[y] = expand(own[y])

    for copy in big:
        copy.wait()
    wide = lax.broadcasted_iota(jnp.int32, (64, 128), 1)
    low = wide < 64
    zero = jnp.zeros((64, 128), F32)

    def put(kind, y, place, first, second):
        rows = pl.ds(place * 64, 64)
        w_v[y, kind, rows, 0:128] = first.astype(BF16)
        w_v[y, kind, rows, 128:256] = second.astype(BF16)

    for y in range(4):
        for side in range(2):
            inv = inv_v[side, y].astype(F32)
            for z in range(2):
                place = 2 * side + z
                block = jnp.where(low if z == 0 else jnp.logical_not(low), inv, 0.0)
                tiles = [block, zero] if side == 0 else [zero, block]
                wb_v[y, pl.ds(place * 64, 64), 0:128] = tiles[0].astype(BF16)
                wb_v[y, pl.ds(place * 64, 64), 128:256] = tiles[1].astype(BF16)

                a = sten_v[side, y, z, :, 0:128].astype(F32)
                b = sten_v[side, y, z, :, 128:256].astype(F32)
                c = sten_v[side, y, z, :, 256:384].astype(F32)
                d = sten_v[side, y, z, :, 384:448].astype(F32)
                d = jnp.concatenate([d, d], axis=1)
                ra, rb, rc = swap(a), swap(b), swap(c)
                if z == 0:
                    centre = jnp.where(low, a, d)
                    toward_o, toward_i = jnp.where(is_odd, b, ra), jnp.where(is_odd, ra, b)
                    toward_m, toward_p = rb, c
                    keep = low
                else:
                    centre = jnp.where(low, rc, ra)
                    toward_o, toward_i = jnp.where(is_odd, rb, a), jnp.where(is_odd, a, rb)
                    toward_m, toward_p = b, rc
                    keep = jnp.logical_not(low)
                toward_o = jnp.where(keep, toward_o, 0.0)
                toward_i = jnp.where(keep, toward_i, 0.0)
                toward_m = jnp.where(keep, toward_m, 0.0)
                toward_p = jnp.where(keep, toward_p, 0.0)
                if side == 0:
                    put(0, y, place, centre, toward_i)
                    put(1, y, place, toward_o, zero)
                    put(2, y, place, toward_m, zero)
                    put(3, y, place, toward_p, zero)
                else:
                    put(0, y, place, toward_o, centre)
                    put(1, y, place, zero, toward_i)
                    put(2, y, place, zero, toward_m)
                    put(3, y, place, zero, toward_p)

    for y in range(4):
        blocks = jnp.concatenate([inv_v[0, y], inv_v[1, y]], axis=1)
        k_v[X_AT[y]] = nn(blocks, w_v[y, 1]).astype(BF16)
        if y in Y_AT:
            k_v[Y_AT[y]] = nn(blocks, w_v[y, 2 if y == 0 else 3]).astype(BF16)

    pl.semaphore_wait(barrier, awaited)
    corner_above = (jnp.logical_and(has_outer, has_above), jnp.logical_and(has_outer, has_below))
    corner_below = (corner_above[1], corner_above[0])
    seeds = [
        send(pack_v.at[:, 3], hy_v.at[0], (gx, above), *to_above),
        send(pack_v.at[0, 3], hd_v.at[0, 0], (outer, above), *corner_above),
        send(pack_v.at[1, 3], hd_v.at[0, 1], (partner, above), *to_above),
        send(pack_v.at[:, 0], hy_v.at[1], (gx, below), *to_below),
        send(pack_v.at[0, 0], hd_v.at[1, 0], (outer, below), *corner_below),
        send(pack_v.at[1, 0], hd_v.at[1, 1], (partner, below), *to_below),
        send(pack_v.at[0], hx_v.at[0], (outer, gy), *to_outer),
        send(pack_v.at[1], hx_v.at[1], (partner, gy)),
    ]
    products = [
        send(k_v.at[4:6], hky_v.at[0], (gx, above), *to_above),
        send(k_v.at[0:2], hky_v.at[1], (gx, below), *to_below),
        send(k_v.at[:, :, 0:128], hkx_v.at[:, :, 0:128], (outer, gy), *to_outer),
        send(k_v.at[:, :, 128:256], hkx_v.at[:, :, 128:256], (partner, gy)),
    ]

    applied = {}
    for y in (3, 0, 1, 2):
        total = nt(st_v[y], w_v[y, 0])
        if y > 0:
            total = total + nt(st_v[y - 1], w_v[y, 2])
        if y < 3:
            total = total + nt(st_v[y + 1], w_v[y, 3])
        applied[y] = total.astype(BF16)
    for y in (3, 0, 1, 2):
        relaxed = nt(applied[y], wb_v[y])
        p0_v[y] = (st_v[y].astype(F32) - RELAX * relaxed).astype(BF16)
    first = [
        send(p0_v.at[3], hp0y_v.at[0], (gx, above), *to_above),
        send(p0_v.at[0], hp0y_v.at[1], (gx, below), *to_below),
        send(p0_v.at[:, :, 0:128], hp0x_v.at[:, :, 0:128], (outer, gy), *to_outer),
        send(p0_v.at[:, :, 128:256], hp0x_v.at[:, :, 128:256], (partner, gy)),
    ]

    await_all(seeds)
    halos, corners = {}, {}
    for end, y in ((1, 3), (0, 0)):
        halos[Y_AT[y]] = jnp.concatenate([hy_v[end, 0], hy_v[end, 1]], axis=1)
        corners[y] = jnp.concatenate([hd_v[end, 0], hd_v[end, 1]], axis=1).astype(F32)
    for y in (3, 0, 1, 2):
        halos[X_AT[y]] = jnp.concatenate([hx_v[0, y], hx_v[1, y]], axis=1)
    applied = {}
    for y in (3, 0, 1, 2):
        applied[y] = nt(halos[X_AT[y]], w_v[y, 1]).astype(BF16)
        if y in Y_AT:
            more = nt(halos[Y_AT[y]], w_v[y, 2 if y == 0 else 3]).astype(BF16)
            applied[y] = jnp.concatenate([applied[y], more], axis=0)
    for y in (3, 0, 1, 2):
        relaxed = nt(applied[y], wb_v[y])
        for n, at in enumerate([X_AT[y]] + ([Y_AT[y]] if y in Y_AT else [])):
            values = -RELAX * relaxed[16 * n : 16 * n + MODES]
            tile = jnp.concatenate([values, halos[at][MODES:].astype(F32)], axis=0)
            pc_v[at] = tile.astype(BF16)

    out[...] = jnp.zeros(out.shape, F32)
    blank = jnp.zeros((64, 128), BF16)
    for y in range(4):
        full = expand(pc_v[X_AT[y]])
        lx_v[y, 0:64, 0:128] = full[:, 0:128]
        lx_v[y, 0:64, 128:256] = blank
        lx_v[y, 64:128, 0:128] = blank
        lx_v[y, 64:128, 128:256] = full[:, 128:256]
        if y in Y_AT:
            lx_v[y, 128:192] = expand(pc_v[Y_AT[y]])

    def left(y, rows):
        return jnp.concatenate([p0_v[y], lx_v[y, 0 : rows - 64]], axis=0)

    ly = {y: by_element(pc_v[Y_AT[y]][0:MODES].astype(F32)) for y in Y_AT}

    terms = [jnp.zeros((rows, 1), F32) for rows in (64, 64, 64, 32, 32)]
    for y in range(4):
        res = jnp.concatenate([res_v[0, y : y + 1, :], res_v[1, y : y + 1, :]], axis=1)
        blocks = [(0, p0_v[y]), (1, lx_v[y, 0:64]), (2, lx_v[y, 64:128])]
        if y in Y_AT:
            blocks.append((3 if y == 0 else 4, ly[y]))
        for slot, block in blocks:
            terms[slot] = terms[slot] + jnp.sum(block.astype(F32) * res, axis=1, keepdims=True)

    for y in range(4):
        size = 256 if y in Y_AT else 192
        acc_v[y, 0:size] = nt(left(y, size), w_v[y, 0])
        if y not in Y_AT:
            acc_v[y, 192:256] = jnp.zeros((64, 256), F32)
        if y > 0:
            size = 256 if y - 1 in Y_AT else 192
            acc_v[y, 0:size] = acc_v[y, 0:size] + nt(left(y - 1, size), w_v[y, 2])
        if y < 3:
            size = 256 if y + 1 in Y_AT else 192
            acc_v[y, 0:size] = acc_v[y, 0:size] + nt(left(y + 1, size), w_v[y, 3])

    await_all(products)
    for y in (3, 0, 1, 2):
        seed, code = own[y][0:MODES], own[y][MODES:]
        fromx = far_slot(seed, code, hkx_v[X_AT[y]])
        if y in Y_AT:
            end = 0 if y == 0 else 1
            far_seed, far_code = corners[y][0:MODES], corners[y][MODES:]
            more = far_slot(far_seed, far_code, hkx_v[Y_AT[y]])
            partx = nt(jnp.concatenate([fromx, more], axis=0), w_v[y, 1])
            fromy = [
                far_slot(far_seed, far_code, hky_v[end, 0]),
                far_slot(seed, code, hky_v[end, 1]),
            ]
            party = nt(jnp.concatenate(fromy, axis=0), w_v[y, 2 + end])
            acc_v[y, 0:64] = acc_v[y, 0:64] + partx[0:64] + party[64:128]
            corner_v[end] = (partx[64:128] + party[0:64]).astype(BF16)
        else:
            acc_v[y, 0:64] = acc_v[y, 0:64] + nt(fromx, w_v[y, 1])

    await_all(first)

    def finish(y):
        part = nt(hp0x_v[y], w_v[y, 1])
        row_0 = acc_v[y, 0:64].astype(BF16)
        row_o, row_i, row_y = acc_v[y, 64:128], acc_v[y, 128:192], acc_v[y, 192:256]
        row_o = jnp.concatenate([row_o[:, 0:128] + part[:, 0:128], row_o[:, 128:256]], axis=1)
        row_i = jnp.concatenate([row_i[:, 0:128], row_i[:, 128:256] + part[:, 128:256]], axis=1)
        row_o, row_i = row_o.astype(BF16), row_i.astype(BF16)
        if y not in Y_AT:
            right = jnp.concatenate([row_0, row_y.astype(BF16), row_i, row_o], axis=0)
            return nt(left(y, 192), right)
        end = 0 if y == 0 else 1
        row_y = (row_y + nt(hp0y_v[end], w_v[y, 2 + end])).astype(BF16)
        corner = corner_v[end]
        corner_o = jnp.concatenate([corner[:, 0:128], blank], axis=1)
        corner_i = jnp.concatenate([blank, corner[:, 128:256]], axis=1)
        right = jnp.concatenate([row_0, row_y, corner_o, row_o, corner_i, row_i], axis=0)
        return nt(jnp.concatenate([left(y, 192), ly[y]], axis=0), right)

    def pick(first, second):
        shape = first.shape if hasattr(first, "shape") else second.shape
        return jnp.where(wide[0 : shape[0]] < 64, first, second)

    def half(tile, near):
        moved = pick(tile, pltpu.roll(tile, 96, 1))
        return jnp.where(is_odd, moved, tile) if near else jnp.where(is_odd, tile, moved)

    def with_terms(tile, term):
        upper = term.astype(BF16).astype(F32)
        at = wide[0 : tile.shape[0]]
        return jnp.where(at == 96, upper, jnp.where(at == 97, term - upper, tile))

    def with_codes(tile, y):
        code = halos[Y_AT[y]][MODES:].astype(F32)
        cells = [code[:, 64 * e : 64 * e + 1] for e in range(4)]
        column = jnp.concatenate(
            [jnp.broadcast_to(cell, (MODES, 128)) for cell in cells], axis=0
        )
        return jnp.where(wide[0:32] == 112, column, tile)

    def tiles(product, slot):
        rows = product[slot * 64 : slot * 64 + 64]
        return [rows[:, 128 * t : 128 * t + 128] for t in range(rows.shape[1] // 128)]

    def post(at, values):
        for n, value in enumerate(values):
            snd_v[at + n] = value.astype(BF16)

    msgs = []
    g3, g0 = finish(3), finish(0)
    for end, g, y, peer, way in ((1, g3, 3, above, to_above), (0, g0, 0, below, to_below)):
        t0, t1, t2 = [g[192:224, 128 * t : 128 * t + 128] for t in range(3)]
        kept = (jnp.where(is_odd, 0.0, t0), t0) if end else (jnp.where(is_odd, t0, 0.0), t0)
        near = half(pick(*kept), True)
        kept = (jnp.where(is_odd, t0, 0.0), t0) if end else (jnp.where(is_odd, 0.0, t0), t0)
        far = half(pick(*kept), False)
        sny_v[end, 0] = with_codes(with_terms(near, terms[3 + end]), y).astype(BF16)
        sny_v[end, 1] = t1.astype(BF16)
        sny_v[end, 2] = with_codes(far, y).astype(BF16)
        sny_v[end, 3] = t2.astype(BF16)
        msgs += [
            send(sny_v.at[end, 0:2], rcy_v.at[1 - end, 0:2], (gx, peer), *way),
            send(sny_v.at[end, 2:4], rcy_v.at[1 - end, 2:4], (partner, peer), *way),
        ]
    g1 = finish(1)
    g2 = finish(2)

    def summed(slot):
        a0, a1, a2 = tiles(g0, slot)
        b0, b1, b2 = tiles(g3, slot)
        c0, c1 = tiles(g1, slot)
        d0, d1 = tiles(g2, slot)
        um, up = a0 + c0, b0 + d0
        mid = c1 + d1
        return um, up, um + up, a1, b1, a1 + b1 + mid, a2, b2, a2 + b2 + swap(mid)

    def by_side(first, second):
        return jnp.where(is_odd, second, first)

    um, up, mid, om, op, o_sum, im, ip, i_sum = summed(1)
    post(
        4,
        [
            with_terms(half(pick(by_side(op, om), o_sum), False), terms[1]),
            pick(mid, up),
            pick(swap(um), i_sum),
        ],
    )
    post(7, [half(pick(by_side(om, op), o_sum), True)])
    msgs += [
        send(snd_v.at[4:7], rcv_v.at[4:7], (outer, gy), *to_outer),
        send(snd_v.at[7:8], rcv_v.at[7:8], (outer2, gy), *to_outer2),
    ]
    um, up, mid, om, op, o_sum, im, ip, i_sum = summed(2)
    post(3, [with_terms(half(pick(by_side(ip, im), i_sum), False), terms[2])])
    far_a = half(pick(by_side(im, ip), i_sum), True)
    far_b = pick(mid, up)
    far_c = pick(swap(um), o_sum)
    um, up, mid, om, op, o_sum, im, ip, i_sum = summed(0)
    post(
        0,
        [
            half(swap(pick(mid, by_side(up, um))), False),
            swap(pick(ip, i_sum)),
            pick(im, 0.0),
        ],
    )
    msgs += [send(snd_v.at[0:4], rcv_v.at[0:4], (partner, gy))]
    own_a = with_terms(half(swap(pick(mid, by_side(um, up))), True), terms[0])
    own_b = swap(pick(op, o_sum))
    own_c = pick(om, 0.0)

    await_all(msgs)

    def got(at):
        return rcv_v[at].astype(F32)

    def spread(end, at):
        first, second = rcy_v[end, at].astype(F32), rcy_v[end, at + 1].astype(F32)
        code = jnp.broadcast_to(first[:, 112:113], (32, 128))
        results = []
        for tile in (first, second):
            rows = []
            for a in range(AGG):
                here = jnp.where(code == float(a), tile, 0.0)
                rows.append(here[0:8] + here[8:16] + here[16:24] + here[24:32])
            results.append(jnp.concatenate(rows, axis=0))
        return results

    (up_a, up_b), (down_a, down_b) = spread(1, 0), spread(0, 0)
    own_a = own_a + got(3) + got(4) + up_a + down_a
    own_b = own_b + got(5) + up_b + pick(down_b, 0.0)
    own_c = own_c + got(6) + pick(swap(down_b), 0.0)
    (up_a, up_b), (down_a, down_b) = spread(1, 2), spread(0, 2)
    far_a = far_a + got(0) + got(7) + up_a + down_a
    far_b = far_b + got(1) + up_b + pick(down_b, 0.0)
    far_c = far_c + got(2) + pick(swap(down_b), 0.0)

    def both(own, far):
        first, second = jnp.where(is_odd, far, own), jnp.where(is_odd, own, far)
        return jnp.concatenate([first, second], axis=0).T

    a, b, c = both(own_a, far_a), both(own_b, far_b), both(own_c, far_c)

    @pl.when(odd == 0)
    def _():
        out[128:192] = c[64:128]
        out[320:384] = c[0:64]
        out[384:512] = b
        out[704:800] = a[0:96]
        out[800:801] = a[96:97] + a[97:98]

    @pl.when(odd == 1)
    def _():
        out[0:32] = a[64:96]
        out[32:96] = a[0:64]
        out[288:352] = c[0:64]
        out[352:480] = b
        out[608:672] = c[64:128]
        out[800:801] = swap(a[96:97] + a[97:98])

    for copy, leaves in sends:
        only(leaves, copy.wait_send)


def finish_kernel(data, coarse, restricted, row, sem):
    first = pltpu.make_async_copy(data.at[pl.ds(0, 800)], coarse.at[0, 0], sem.at[0])
    first.start()
    row[...] = data[800:801, 0:64]
    second = pltpu.make_async_copy(row, restricted.at[0], sem.at[1])
    second.start()
    first.wait()
    second.wait()


def body(stencil, inverse, tentative, aggregate, residual):
    hbm = pl.BlockSpec(memory_space=pltpu.HBM)
    aggregate = aggregate.transpose(0, 2, 1)
    operands = [
        pltpu.with_memory_space_constraint(operand, pltpu.HBM)
        for operand in (stencil, inverse, tentative, aggregate, residual)
    ]
    vmem = pl.BlockSpec(memory_space=pltpu.VMEM)
    scratch = [
        pltpu.VMEM(stencil.shape, BF16),
        pltpu.VMEM(inverse.shape, BF16),
        pltpu.VMEM(tentative.shape, BF16),
        pltpu.VMEM(aggregate.shape, jnp.int32),
        pltpu.VMEM(residual.shape, F32),
        pltpu.VMEM((4, 4, 256, 256), BF16),
        pltpu.VMEM((4, 256, 256), BF16),
        pltpu.VMEM((2, 4, 16, 128), BF16),
        pltpu.VMEM((2, 4, 16, 128), BF16),
        pltpu.VMEM((2, 2, 16, 128), BF16),
        pltpu.VMEM((2, 2, 16, 128), BF16),
        pltpu.VMEM((6, 64, 256), BF16),
        pltpu.VMEM((6, 64, 256), BF16),
        pltpu.VMEM((2, 2, 64, 256), BF16),
        pltpu.VMEM((4, 64, 256), BF16),
        pltpu.VMEM((4, 64, 256), BF16),
        pltpu.VMEM((2, 64, 256), BF16),
        pltpu.VMEM((6, 16, 256), BF16),
        pltpu.VMEM((2, 64, 256), BF16),
        pltpu.VMEM((4, 64, 256), BF16),
        pltpu.VMEM((4, 192, 256), BF16),
        pltpu.VMEM((4, 256, 256), F32),
        pltpu.VMEM((8, 64, 128), BF16),
        pltpu.VMEM((8, 64, 128), BF16),
        pltpu.VMEM((2, 4, 32, 128), BF16),
        pltpu.VMEM((2, 4, 32, 128), BF16),
        pltpu.SemaphoreType.DMA((10,)),
        pltpu.SemaphoreType.DMA((23,)),
        pltpu.SemaphoreType.DMA((23,)),
    ]
    sizes = (lax.axis_size("gx"), lax.axis_size("gy"))

    def call(*refs):
        kernel(*sizes, *refs)

    coarse = pl.pallas_call(
        call,
        out_shape=pltpu.VMEM((808, 128), F32),
        in_specs=[hbm] * 5,
        out_specs=vmem,
        scratch_shapes=scratch,
        compiler_params=pltpu.CompilerParams(
            collective_id=0, has_side_effects=True, vmem_limit_bytes=32 << 20
        ),
        name="galerkin",
    )(*operands)
    coarse, restricted = pl.pallas_call(
        finish_kernel,
        out_shape=(
            jax.ShapeDtypeStruct((1, 1, 800, 128), F32),
            jax.ShapeDtypeStruct((1, 1, 64), F32),
        ),
        in_specs=[pl.BlockSpec(memory_space=pltpu.VMEM)],
        out_specs=(pl.BlockSpec(memory_space=pl.ANY), pl.BlockSpec(memory_space=pl.ANY)),
        scratch_shapes=[pltpu.VMEM((1, 64), F32), pltpu.SemaphoreType.DMA((2,))],
        name="store",
    )(pltpu.with_memory_space_constraint(coarse, pltpu.VMEM))
    return coarse.swapaxes(2, 3), restricted


def solution(mesh):
    in_specs = (
        P("gx", "gy", None, None, None),
        P("gx", "gy", None, None),
        P("gx", "gy", None, None),
        P("gx", "gy", None),
        P("gx", "gy", None),
    )
    out_specs = (P("gx", "gy", None, None), P("gx", "gy", None))
    return jax.shard_map(body, mesh=mesh, in_specs=in_specs, out_specs=out_specs, check_vma=False)
```

```python
import jax
import jax.numpy as jnp
from jax import lax
from jax.experimental import pallas as pl
from jax.experimental.pallas import tpu as pltpu
from jax.sharding import PartitionSpec as P

MESH = pl.DeviceIdType.MESH
F32, BF16 = jnp.float32, jnp.bfloat16
AGG = 8
MODES = 8
RELAX = 0.6


X_AT, Y_AT = (0, 2, 3, 4), {0: 1, 3: 5}


def nt(left, right):
    return lax.dot_general(left, right, (((1,), (1,)), ((), ())), preferred_element_type=F32)


def nn(left, right):
    return lax.dot_general(left, right, (((1,), (0,)), ((), ())), preferred_element_type=F32)


def spread_columns(values, code):
    rows = [jnp.where(code == float(a), values, 0.0) for a in range(AGG)]
    return jnp.concatenate(rows, axis=0).astype(BF16)


def expand(tile):
    return spread_columns(tile[0:MODES].astype(F32), tile[MODES : 2 * MODES].astype(F32))


def by_element(values):
    lane = lax.broadcasted_iota(jnp.int32, (MODES, 256), 1)
    parts = [
        jnp.where(jnp.logical_and(lane >= 64 * e, lane < 64 * e + 64), values, 0.0)
        for e in range(4)
    ]
    return jnp.concatenate(parts, axis=0).astype(BF16)


def slot_values(seeds, product):
    rows = -RELAX * nt(seeds, product)
    values = jnp.concatenate([rows[8 * e : 8 * e + 8] for e in range(4)], axis=1)
    return values.astype(BF16).astype(F32)


def swap(tile):
    return pltpu.roll(tile, 64, 1)


def kernel(
    n_gx,
    n_gy,
    stencil,
    inverse,
    tentative,
    aggregate,
    residual,
    out,
    sten_v,
    inv_v,
    tent_v,
    agg_v,
    res_v,
    w_v,
    wb_v,
    pack_v,
    hx_v,
    hy_v,
    hd_v,
    k_v,
    hkx_v,
    hky_v,
    p0_v,
    hp0x_v,
    hp0y_v,
    st_v,
    lx_v,
    acc_v,
    snd_v,
    rcv_v,
    sny_v,
    rcy_v,
    load_sem,
    send_sem,
    recv_sem,
):
    gx, gy = lax.axis_index("gx"), lax.axis_index("gy")
    odd = lax.rem(gx, 2)
    is_odd = odd == 1
    turn = 2 * odd - 1
    partner = gx - turn
    outer = lax.rem(gx + turn + n_gx, n_gx)
    outer2 = lax.rem(gx + 2 * turn + n_gx, n_gx)
    back2 = lax.rem(gx - 2 * turn + n_gx, n_gx)
    below = lax.rem(gy - 1 + n_gy, n_gy)
    above = lax.rem(gy + 1, n_gy)
    has_outer = jnp.logical_and(gx > 0, gx < n_gx - 1)
    has_back = jnp.logical_and(partner > 0, partner < n_gx - 1)
    has_below, has_above = gy > 0, gy < n_gy - 1

    def only(condition, action):
        if condition is None:
            action()
        else:
            pl.when(condition)(action)

    barrier = pltpu.get_barrier_semaphore()
    peers = [
        ((gx, above), has_above),
        ((partner, above), has_above),
        ((outer, above), jnp.logical_and(has_outer, has_above)),
        ((gx, below), has_below),
        ((partner, below), has_below),
        ((outer, below), jnp.logical_and(has_outer, has_below)),
        ((outer, gy), has_outer),
        ((outer2, gy), has_outer),
        ((back2, gy), has_back),
        ((partner, gy), None),
    ]
    for peer, condition in peers:
        only(
            condition,
            lambda peer=peer: pl.semaphore_signal(
                barrier, inc=1, device_id=peer, device_id_type=MESH
            ),
        )
    awaited = 1
    for _, condition in peers[:-1]:
        awaited = awaited + jnp.where(condition, 1, 0)

    loads = []

    def load(src, dst):
        copy = pltpu.make_async_copy(src, dst, load_sem.at[len(loads)])
        copy.start()
        loads.append(copy)
        return copy

    small = []
    for side in range(2):
        x = side + odd - 2 * side * odd
        small.append(load(tentative.at[x], tent_v.at[side]))
        small.append(load(aggregate.at[x], agg_v.at[side]))
    big = []
    for side in range(2):
        x = side + odd - 2 * side * odd
        big.append(load(stencil.at[x], sten_v.at[side]))
        big.append(load(inverse.at[x], inv_v.at[side]))
        big.append(load(residual.at[x], res_v.at[side]))

    sends = []

    def send(src, dst, peer, leaves=None, arrives=None):
        at = len(sends)
        copy = pltpu.make_async_remote_copy(
            src_ref=src,
            dst_ref=dst,
            send_sem=send_sem.at[at],
            recv_sem=recv_sem.at[at],
            device_id=peer,
            device_id_type=MESH,
        )
        only(leaves, copy.start)
        sends.append((copy, leaves))
        return copy, arrives

    def await_all(copies):
        for copy, arrives in copies:
            only(arrives, copy.wait_recv)

    to_outer, to_outer2 = (has_outer, has_outer), (has_outer, has_back)
    to_below, to_above = (has_below, has_above), (has_above, has_below)

    @pl.when(jnp.logical_not(has_outer))
    def _():
        hx_v[0] = jnp.zeros(hx_v.shape[1:], BF16)
        hd_v[:, 0] = jnp.zeros((2, 16, 128), BF16)
        hkx_v[:, :, 0:128] = jnp.zeros((6, 64, 128), BF16)
        hp0x_v[:, :, 0:128] = jnp.zeros((4, 64, 128), BF16)
        rcv_v[4:7] = jnp.zeros((3, 64, 128), BF16)

    @pl.when(jnp.logical_not(has_back))
    def _():
        rcv_v[7] = jnp.zeros((64, 128), BF16)

    for end, condition in enumerate((has_below, has_above)):

        @pl.when(jnp.logical_not(condition))
        def _(end=end):
            hy_v[end] = jnp.zeros((2, 16, 128), BF16)
            hd_v[end] = jnp.zeros((2, 16, 128), BF16)
            hky_v[end] = jnp.zeros((2, 64, 256), BF16)
            hp0y_v[end] = jnp.zeros((64, 256), BF16)
            rcy_v[end] = jnp.zeros((4, 32, 128), BF16)

    lane = lax.broadcasted_iota(jnp.int32, (8, 128), 1)
    def packed(modes, code_0, code_1):
        code = jnp.where(
            lane < 64, jnp.broadcast_to(code_0, (8, 128)), jnp.broadcast_to(code_1, (8, 128))
        )
        return jnp.concatenate([modes.astype(F32), code.astype(F32)], axis=0).astype(BF16)

    for copy in small:
        copy.wait()

    own = {}
    for y in range(4):
        row = pl.ds(y, 1)
        tiles = []
        for side in range(2):
            tile = packed(tent_v[side, y], agg_v[side, 0:1, row], agg_v[side, 1:2, row])
            pack_v[side, y] = tile
            tiles.append(tile)
        own[y] = jnp.concatenate(tiles, axis=1).astype(F32)
        st_v[y] = expand(own[y])

    for copy in big:
        copy.wait()
    wide = lax.broadcasted_iota(jnp.int32, (64, 128), 1)
    low = wide < 64
    zero = jnp.zeros((64, 128), F32)

    def put(kind, y, place, first, second):
        rows = pl.ds(place * 64, 64)
        w_v[y, kind, rows, 0:128] = first.astype(BF16)
        w_v[y, kind, rows, 128:256] = second.astype(BF16)

    for y in range(4):
        for side in range(2):
            inv = inv_v[side, y].astype(F32)
            for z in range(2):
                place = 2 * side + z
                block = jnp.where(low if z == 0 else jnp.logical_not(low), inv, 0.0)
                tiles = [block, zero] if side == 0 else [zero, block]
                wb_v[y, pl.ds(place * 64, 64), 0:128] = tiles[0].astype(BF16)
                wb_v[y, pl.ds(place * 64, 64), 128:256] = tiles[1].astype(BF16)

                a = sten_v[side, y, z, :, 0:128].astype(F32)
                b = sten_v[side, y, z, :, 128:256].astype(F32)
                c = sten_v[side, y, z, :, 256:384].astype(F32)
                d = sten_v[side, y, z, :, 384:448].astype(F32)
                d = jnp.concatenate([d, d], axis=1)
                ra, rb, rc = swap(a), swap(b), swap(c)
                if z == 0:
                    centre = jnp.where(low, a, d)
                    toward_o, toward_i = jnp.where(is_odd, b, ra), jnp.where(is_odd, ra, b)
                    toward_m, toward_p = rb, c
                    keep = low
                else:
                    centre = jnp.where(low, rc, ra)
                    toward_o, toward_i = jnp.where(is_odd, rb, a), jnp.where(is_odd, a, rb)
                    toward_m, toward_p = b, rc
                    keep = jnp.logical_not(low)
                toward_o = jnp.where(keep, toward_o, 0.0)
                toward_i = jnp.where(keep, toward_i, 0.0)
                toward_m = jnp.where(keep, toward_m, 0.0)
                toward_p = jnp.where(keep, toward_p, 0.0)
                if side == 0:
                    put(0, y, place, centre, toward_i)
                    put(1, y, place, toward_o, zero)
                    put(2, y, place, toward_m, zero)
                    put(3, y, place, toward_p, zero)
                else:
                    put(0, y, place, toward_o, centre)
                    put(1, y, place, zero, toward_i)
                    put(2, y, place, zero, toward_m)
                    put(3, y, place, zero, toward_p)

    for y in range(4):
        blocks = jnp.concatenate([inv_v[0, y], inv_v[1, y]], axis=1)
        k_v[X_AT[y]] = nn(blocks, w_v[y, 1]).astype(BF16)
        if y in Y_AT:
            k_v[Y_AT[y]] = nn(blocks, w_v[y, 2 if y == 0 else 3]).astype(BF16)

    applied = {}
    for y in (3, 0, 1, 2):
        total = nt(st_v[y], w_v[y, 0])
        if y > 0:
            total = total + nt(st_v[y - 1], w_v[y, 2])
        if y < 3:
            total = total + nt(st_v[y + 1], w_v[y, 3])
        applied[y] = total.astype(BF16)
    for y in (3, 0, 1, 2):
        relaxed = nt(applied[y], wb_v[y])
        p0_v[y] = (st_v[y].astype(F32) - RELAX * relaxed).astype(BF16)
    pl.semaphore_wait(barrier, awaited)
    corner_above = (jnp.logical_and(has_outer, has_above), jnp.logical_and(has_outer, has_below))
    corner_below = (corner_above[1], corner_above[0])
    seeds = [
        send(pack_v.at[:, 3], hy_v.at[0], (gx, above), *to_above),
        send(pack_v.at[0, 3], hd_v.at[0, 0], (outer, above), *corner_above),
        send(pack_v.at[1, 3], hd_v.at[0, 1], (partner, above), *to_above),
        send(pack_v.at[:, 0], hy_v.at[1], (gx, below), *to_below),
        send(pack_v.at[0, 0], hd_v.at[1, 0], (outer, below), *corner_below),
        send(pack_v.at[1, 0], hd_v.at[1, 1], (partner, below), *to_below),
        send(pack_v.at[0], hx_v.at[0], (outer, gy), *to_outer),
        send(pack_v.at[1], hx_v.at[1], (partner, gy)),
    ]
    products = [
        send(k_v.at[4:6], hky_v.at[0], (gx, above), *to_above),
        send(k_v.at[0:2], hky_v.at[1], (gx, below), *to_below),
        send(k_v.at[:, :, 0:128], hkx_v.at[:, :, 0:128], (outer, gy), *to_outer),
        send(k_v.at[:, :, 128:256], hkx_v.at[:, :, 128:256], (partner, gy)),
    ]

    first = [
        send(p0_v.at[3], hp0y_v.at[0], (gx, above), *to_above),
        send(p0_v.at[0], hp0y_v.at[1], (gx, below), *to_below),
        send(p0_v.at[:, :, 0:128], hp0x_v.at[:, :, 0:128], (outer, gy), *to_outer),
        send(p0_v.at[:, :, 128:256], hp0x_v.at[:, :, 128:256], (partner, gy)),
    ]

    out[...] = jnp.zeros(out.shape, F32)
    seeds_by = {y: by_element(own[y][0:MODES]) for y in range(4)}
    blank = jnp.zeros((64, 128), BF16)

    await_all(seeds)
    halos, corners = {}, {}
    for end, y in ((1, 3), (0, 0)):
        halos[Y_AT[y]] = jnp.concatenate([hy_v[end, 0], hy_v[end, 1]], axis=1).astype(F32)
        corners[y] = jnp.concatenate([hd_v[end, 0], hd_v[end, 1]], axis=1).astype(F32)
    for y in range(4):
        halos[X_AT[y]] = jnp.concatenate([hx_v[0, y], hx_v[1, y]], axis=1).astype(F32)
    values = {at: slot_values(by_element(halos[at][0:MODES]), k_v[at]) for at in halos}
    full = {at: spread_columns(values[at], halos[at][MODES:]) for at in halos}
    corners_by = {y: by_element(corners[y][0:MODES]) for y in Y_AT}
    ly = {y: by_element(values[Y_AT[y]]) for y in Y_AT}
    for y in range(4):
        slot = full[X_AT[y]]
        lx_v[y, 0:64, 0:128] = slot[:, 0:128]
        lx_v[y, 0:64, 128:256] = blank
        lx_v[y, 64:128, 0:128] = blank
        lx_v[y, 64:128, 128:256] = slot[:, 128:256]
        if y in Y_AT:
            lx_v[y, 128:192] = full[Y_AT[y]]

    def left(y, rows):
        return jnp.concatenate([p0_v[y], lx_v[y, 0 : rows - 64]], axis=0)

    terms = [jnp.zeros((rows, 1), F32) for rows in (64, 64, 64, 32, 32)]
    for y in range(4):
        res = jnp.concatenate([res_v[0, y : y + 1, :], res_v[1, y : y + 1, :]], axis=1)
        blocks = [(0, p0_v[y]), (1, lx_v[y, 0:64]), (2, lx_v[y, 64:128])]
        if y in Y_AT:
            blocks.append((3 if y == 0 else 4, ly[y]))
        for slot, block in blocks:
            terms[slot] = terms[slot] + jnp.sum(block.astype(F32) * res, axis=1, keepdims=True)

    for y in range(4):
        size = 256 if y in Y_AT else 192
        acc_v[y, 0:size] = nt(left(y, size), w_v[y, 0])
        if y not in Y_AT:
            acc_v[y, 192:256] = jnp.zeros((64, 256), F32)
        if y > 0:
            size = 256 if y - 1 in Y_AT else 192
            acc_v[y, 0:size] = acc_v[y, 0:size] + nt(left(y - 1, size), w_v[y, 2])
        if y < 3:
            size = 256 if y + 1 in Y_AT else 192
            acc_v[y, 0:size] = acc_v[y, 0:size] + nt(left(y + 1, size), w_v[y, 3])

    await_all(products)
    near_x, near_y, far_x, far_y = {}, {}, {}, {}
    for y in (3, 0, 1, 2):
        near_x[y] = slot_values(seeds_by[y], hkx_v[X_AT[y]])
    for end, y in ((1, 3), (0, 0)):
        near_y[y] = slot_values(seeds_by[y], hky_v[end, 1])
        far_x[y] = slot_values(corners_by[y], hkx_v[Y_AT[y]])
        far_y[y] = slot_values(corners_by[y], hky_v[end, 0])
    near_x = {y: spread_columns(near_x[y], own[y][MODES:]) for y in range(4)}
    near_y = {y: spread_columns(near_y[y], own[y][MODES:]) for y in Y_AT}
    far_x = {y: spread_columns(far_x[y], corners[y][MODES:]) for y in Y_AT}
    far_y = {y: spread_columns(far_y[y], corners[y][MODES:]) for y in Y_AT}

    await_all(first)

    def coupled(y):
        rows = [hp0x_v[y], near_x[y]] + ([far_x[y]] if y in Y_AT else [])
        part = nt(jnp.concatenate(rows, axis=0), w_v[y, 1])
        row_0 = acc_v[y, 0:64] + part[64:128]
        row_o, row_i, row_y = acc_v[y, 64:128], acc_v[y, 128:192], acc_v[y, 192:256]
        row_o = jnp.concatenate([row_o[:, 0:128] + part[0:64, 0:128], row_o[:, 128:256]], axis=1)
        row_i = jnp.concatenate([row_i[:, 0:128], row_i[:, 128:256] + part[0:64, 128:256]], axis=1)
        row_o, row_i = row_o.astype(BF16), row_i.astype(BF16)
        if y not in Y_AT:
            rows = [row_0.astype(BF16), row_y.astype(BF16), row_i, row_o]
            return jnp.concatenate(rows, axis=0)
        end = 0 if y == 0 else 1
        rows = [hp0y_v[end], far_y[y], near_y[y]]
        more = nt(jnp.concatenate(rows, axis=0), w_v[y, 2 + end])
        row_0, row_y = (row_0 + more[128:192]).astype(BF16), (row_y + more[0:64]).astype(BF16)
        corner = (part[128:192] + more[64:128]).astype(BF16)
        corner_o = jnp.concatenate([corner[:, 0:128], blank], axis=1)
        corner_i = jnp.concatenate([blank, corner[:, 128:256]], axis=1)
        return jnp.concatenate([row_0, row_y, corner_o, row_o, corner_i, row_i], axis=0)

    right = {y: coupled(y) for y in (3, 0, 1, 2)}
    g3 = nt(jnp.concatenate([left(3, 192), ly[3]], axis=0), right[3])
    g0 = nt(jnp.concatenate([left(0, 192), ly[0]], axis=0), right[0])
    g1 = nt(left(1, 192), right[1])
    g2 = nt(left(2, 192), right[2])

    def pick(first, second):
        shape = first.shape if hasattr(first, "shape") else second.shape
        return jnp.where(wide[0 : shape[0]] < 64, first, second)

    def half(tile, near):
        moved = pick(tile, pltpu.roll(tile, 96, 1))
        return jnp.where(is_odd, moved, tile) if near else jnp.where(is_odd, tile, moved)

    def with_terms(tile, term):
        upper = term.astype(BF16).astype(F32)
        at = wide[0 : tile.shape[0]]
        return jnp.where(at == 96, upper, jnp.where(at == 97, term - upper, tile))

    def with_codes(tile, y):
        code = halos[Y_AT[y]][MODES:]
        cells = [code[:, 64 * e : 64 * e + 1] for e in range(4)]
        column = jnp.concatenate(
            [jnp.broadcast_to(cell, (MODES, 128)) for cell in cells], axis=0
        )
        return jnp.where(wide[0:32] == 112, column, tile)

    def tiles(product, slot):
        rows = product[slot * 64 : slot * 64 + 64]
        return [rows[:, 128 * t : 128 * t + 128] for t in range(rows.shape[1] // 128)]

    def post(at, values):
        for n, value in enumerate(values):
            snd_v[at + n] = value.astype(BF16)

    msgs = []
    for end, g, y, peer, way in ((1, g3, 3, above, to_above), (0, g0, 0, below, to_below)):
        t0, t1, t2 = [g[192:224, 128 * t : 128 * t + 128] for t in range(3)]
        kept = (jnp.where(is_odd, 0.0, t0), t0) if end else (jnp.where(is_odd, t0, 0.0), t0)
        near = half(pick(*kept), True)
        kept = (jnp.where(is_odd, t0, 0.0), t0) if end else (jnp.where(is_odd, 0.0, t0), t0)
        far = half(pick(*kept), False)
        sny_v[end, 0] = with_codes(with_terms(near, terms[3 + end]), y).astype(BF16)
        sny_v[end, 1] = t1.astype(BF16)
        sny_v[end, 2] = with_codes(far, y).astype(BF16)
        sny_v[end, 3] = t2.astype(BF16)
        msgs += [
            send(sny_v.at[end, 0:2], rcy_v.at[1 - end, 0:2], (gx, peer), *way),
            send(sny_v.at[end, 2:4], rcy_v.at[1 - end, 2:4], (partner, peer), *way),
        ]

    def summed(slot):
        a0, a1, a2 = tiles(g0, slot)
        b0, b1, b2 = tiles(g3, slot)
        c0, c1 = tiles(g1, slot)
        d0, d1 = tiles(g2, slot)
        um, up = a0 + c0, b0 + d0
        mid = c1 + d1
        return um, up, um + up, a1, b1, a1 + b1 + mid, a2, b2, a2 + b2 + swap(mid)

    def by_side(first, second):
        return jnp.where(is_odd, second, first)

    um, up, mid, om, op, o_sum, im, ip, i_sum = summed(1)
    post(
        4,
        [
            with_terms(half(pick(by_side(op, om), o_sum), False), terms[1]),
            pick(mid, up),
            pick(swap(um), i_sum),
        ],
    )
    post(7, [half(pick(by_side(om, op), o_sum), True)])
    msgs += [
        send(snd_v.at[4:7], rcv_v.at[4:7], (outer, gy), *to_outer),
        send(snd_v.at[7:8], rcv_v.at[7:8], (outer2, gy), *to_outer2),
    ]
    um, up, mid, om, op, o_sum, im, ip, i_sum = summed(2)
    post(3, [with_terms(half(pick(by_side(ip, im), i_sum), False), terms[2])])
    far_a = half(pick(by_side(im, ip), i_sum), True)
    far_b = pick(mid, up)
    far_c = pick(swap(um), o_sum)
    um, up, mid, om, op, o_sum, im, ip, i_sum = summed(0)
    post(
        0,
        [
            half(swap(pick(mid, by_side(up, um))), False),
            swap(pick(ip, i_sum)),
            pick(im, 0.0),
        ],
    )
    msgs += [send(snd_v.at[0:4], rcv_v.at[0:4], (partner, gy))]
    own_a = with_terms(half(swap(pick(mid, by_side(um, up))), True), terms[0])
    own_b = swap(pick(op, o_sum))
    own_c = pick(om, 0.0)

    def got(at):
        return rcv_v[at].astype(F32)

    def spread(end, at):
        first, second = rcy_v[end, at].astype(F32), rcy_v[end, at + 1].astype(F32)
        code = jnp.broadcast_to(first[:, 112:113], (32, 128))
        results = []
        for tile in (first, second):
            rows = []
            for a in range(AGG):
                here = jnp.where(code == float(a), tile, 0.0)
                rows.append(here[0:8] + here[8:16] + here[16:24] + here[24:32])
            results.append(jnp.concatenate(rows, axis=0))
        return results

    await_all(msgs[6:7])
    own_a, far_a = own_a + got(3), far_a + got(0)
    far_b, far_c = far_b + got(1), far_c + got(2)
    await_all(msgs[2:4])
    (near_a, near_b), (past_a, past_b) = spread(1, 0), spread(1, 2)
    own_a, own_b = own_a + near_a, own_b + near_b
    far_a, far_b = far_a + past_a, far_b + past_b
    await_all(msgs[4:6])
    own_a, own_b, own_c = own_a + got(4), own_b + got(5), own_c + got(6)
    far_a = far_a + got(7)
    await_all(msgs[0:2])
    (near_a, near_b), (past_a, past_b) = spread(0, 0), spread(0, 2)
    own_a, own_b = own_a + near_a, own_b + pick(near_b, 0.0)
    own_c = own_c + pick(swap(near_b), 0.0)
    far_a, far_b = far_a + past_a, far_b + pick(past_b, 0.0)
    far_c = far_c + pick(swap(past_b), 0.0)

    def both(own, far):
        first, second = jnp.where(is_odd, far, own), jnp.where(is_odd, own, far)
        return jnp.concatenate([first, second], axis=0).T

    a, b, c = both(own_a, far_a), both(own_b, far_b), both(own_c, far_c)

    @pl.when(odd == 0)
    def _():
        out[128:192] = c[64:128]
        out[320:384] = c[0:64]
        out[384:512] = b
        out[704:800] = a[0:96]
        out[800:801] = a[96:97] + a[97:98]

    @pl.when(odd == 1)
    def _():
        out[0:32] = a[64:96]
        out[32:96] = a[0:64]
        out[288:352] = c[0:64]
        out[352:480] = b
        out[608:672] = c[64:128]
        out[800:801] = swap(a[96:97] + a[97:98])

    for copy, leaves in sends:
        only(leaves, copy.wait_send)


def finish_kernel(data, coarse, restricted, row, sem):
    first = pltpu.make_async_copy(data.at[pl.ds(0, 800)], coarse.at[0, 0], sem.at[0])
    first.start()
    row[...] = data[800:801, 0:64]
    second = pltpu.make_async_copy(row, restricted.at[0], sem.at[1])
    second.start()
    first.wait()
    second.wait()


def body(stencil, inverse, tentative, aggregate, residual):
    hbm = pl.BlockSpec(memory_space=pltpu.HBM)
    aggregate = aggregate.transpose(0, 2, 1)
    operands = [
        pltpu.with_memory_space_constraint(operand, pltpu.HBM)
        for operand in (stencil, inverse, tentative, aggregate, residual)
    ]
    vmem = pl.BlockSpec(memory_space=pltpu.VMEM)
    scratch = [
        pltpu.VMEM(stencil.shape, BF16),
        pltpu.VMEM(inverse.shape, BF16),
        pltpu.VMEM(tentative.shape, BF16),
        pltpu.VMEM(aggregate.shape, jnp.int32),
        pltpu.VMEM(residual.shape, F32),
        pltpu.VMEM((4, 4, 256, 256), BF16),
        pltpu.VMEM((4, 256, 256), BF16),
        pltpu.VMEM((2, 4, 16, 128), BF16),
        pltpu.VMEM((2, 4, 16, 128), BF16),
        pltpu.VMEM((2, 2, 16, 128), BF16),
        pltpu.VMEM((2, 2, 16, 128), BF16),
        pltpu.VMEM((6, 64, 256), BF16),
        pltpu.VMEM((6, 64, 256), BF16),
        pltpu.VMEM((2, 2, 64, 256), BF16),
        pltpu.VMEM((4, 64, 256), BF16),
        pltpu.VMEM((4, 64, 256), BF16),
        pltpu.VMEM((2, 64, 256), BF16),
        pltpu.VMEM((4, 64, 256), BF16),
        pltpu.VMEM((4, 192, 256), BF16),
        pltpu.VMEM((4, 256, 256), F32),
        pltpu.VMEM((8, 64, 128), BF16),
        pltpu.VMEM((8, 64, 128), BF16),
        pltpu.VMEM((2, 4, 32, 128), BF16),
        pltpu.VMEM((2, 4, 32, 128), BF16),
        pltpu.SemaphoreType.DMA((10,)),
        pltpu.SemaphoreType.DMA((23,)),
        pltpu.SemaphoreType.DMA((23,)),
    ]
    sizes = (lax.axis_size("gx"), lax.axis_size("gy"))

    def call(*refs):
        kernel(*sizes, *refs)

    coarse = pl.pallas_call(
        call,
        out_shape=pltpu.VMEM((808, 128), F32),
        in_specs=[hbm] * 5,
        out_specs=vmem,
        scratch_shapes=scratch,
        compiler_params=pltpu.CompilerParams(
            collective_id=0, has_side_effects=True, vmem_limit_bytes=32 << 20
        ),
        name="galerkin",
    )(*operands)
    coarse, restricted = pl.pallas_call(
        finish_kernel,
        out_shape=(
            jax.ShapeDtypeStruct((1, 1, 800, 128), F32),
            jax.ShapeDtypeStruct((1, 1, 64), F32),
        ),
        in_specs=[pl.BlockSpec(memory_space=pltpu.VMEM)],
        out_specs=(pl.BlockSpec(memory_space=pl.ANY), pl.BlockSpec(memory_space=pl.ANY)),
        scratch_shapes=[pltpu.VMEM((1, 64), F32), pltpu.SemaphoreType.DMA((2,))],
        name="store",
    )(pltpu.with_memory_space_constraint(coarse, pltpu.VMEM))
    return coarse.swapaxes(2, 3), restricted


def solution(mesh):
    in_specs = (
        P("gx", "gy", None, None, None),
        P("gx", "gy", None, None),
        P("gx", "gy", None, None),
        P("gx", "gy", None),
        P("gx", "gy", None),
    )
    out_specs = (P("gx", "gy", None, None), P("gx", "gy", None))
    return jax.shard_map(body, mesh=mesh, in_specs=in_specs, out_specs=out_specs, check_vma=False)
```

```python
import jax
import jax.numpy as jnp
from jax import lax
from jax.experimental import pallas as pl
from jax.experimental.pallas import tpu as pltpu
from jax.sharding import PartitionSpec as P

MESH = pl.DeviceIdType.MESH
F32, BF16 = jnp.float32, jnp.bfloat16
AGG = 8
MODES = 8
RELAX = 0.6


X_AT, Y_AT = (0, 2, 3, 4), {0: 1, 3: 5}


def nt(left, right):
    return lax.dot_general(left, right, (((1,), (1,)), ((), ())), preferred_element_type=F32)


def nn(left, right):
    return lax.dot_general(left, right, (((1,), (0,)), ((), ())), preferred_element_type=F32)


def spread_columns(values, code):
    rows = [jnp.where(code == float(a), values, 0.0) for a in range(AGG)]
    return jnp.concatenate(rows, axis=0).astype(BF16)


def expand(tile):
    return spread_columns(tile[0:MODES].astype(F32), tile[MODES : 2 * MODES].astype(F32))


def by_element(values):
    lane = lax.broadcasted_iota(jnp.int32, (MODES, 256), 1)
    parts = [
        jnp.where(jnp.logical_and(lane >= 64 * e, lane < 64 * e + 64), values, 0.0)
        for e in range(4)
    ]
    return jnp.concatenate(parts, axis=0).astype(BF16)


def slot_values(seeds, product):
    rows = -RELAX * nt(seeds, product)
    values = jnp.concatenate([rows[8 * e : 8 * e + 8] for e in range(4)], axis=1)
    return values.astype(BF16).astype(F32)


def halves(ref, at, dim=0):
    parts = [ref[at, n] if dim else ref[n, at] for n in range(2)]
    return jnp.concatenate(parts, axis=1)


def put_halves(ref, at, value):
    ref[0, at] = value[:, 0:128].astype(BF16)
    ref[1, at] = value[:, 128:256].astype(BF16)


def swap(tile):
    return pltpu.roll(tile, 64, 1)


def kernel(
    n_gx,
    n_gy,
    stencil,
    inverse,
    tentative,
    aggregate,
    residual,
    out,
    sten_v,
    inv_v,
    tent_v,
    agg_v,
    res_v,
    w_v,
    wb_v,
    pack_v,
    hx_v,
    hy_v,
    hd_v,
    k_v,
    hkx_v,
    hky_v,
    p0_v,
    hp0x_v,
    hp0y_v,
    st_v,
    lx_v,
    acc_v,
    snd_v,
    rcv_v,
    sny_v,
    rcy_v,
    load_sem,
    send_sem,
    recv_sem,
):
    gx, gy = lax.axis_index("gx"), lax.axis_index("gy")
    odd = lax.rem(gx, 2)
    is_odd = odd == 1
    turn = 2 * odd - 1
    partner = gx - turn
    outer = lax.rem(gx + turn + n_gx, n_gx)
    outer2 = lax.rem(gx + 2 * turn + n_gx, n_gx)
    back2 = lax.rem(gx - 2 * turn + n_gx, n_gx)
    below = lax.rem(gy - 1 + n_gy, n_gy)
    above = lax.rem(gy + 1, n_gy)
    has_outer = jnp.logical_and(gx > 0, gx < n_gx - 1)
    has_back = jnp.logical_and(partner > 0, partner < n_gx - 1)
    has_below, has_above = gy > 0, gy < n_gy - 1

    def only(condition, action):
        if condition is None:
            action()
        else:
            pl.when(condition)(action)

    barrier = pltpu.get_barrier_semaphore()
    peers = [
        ((gx, above), has_above),
        ((partner, above), has_above),
        ((outer, above), jnp.logical_and(has_outer, has_above)),
        ((gx, below), has_below),
        ((partner, below), has_below),
        ((outer, below), jnp.logical_and(has_outer, has_below)),
        ((outer, gy), has_outer),
        ((outer2, gy), has_outer),
        ((back2, gy), has_back),
        ((partner, gy), None),
    ]
    for peer, condition in peers:
        only(
            condition,
            lambda peer=peer: pl.semaphore_signal(
                barrier, inc=1, device_id=peer, device_id_type=MESH
            ),
        )
    awaited = 1
    for _, condition in peers[:-1]:
        awaited = awaited + jnp.where(condition, 1, 0)

    loads = []

    def load(src, dst):
        copy = pltpu.make_async_copy(src, dst, load_sem.at[len(loads)])
        copy.start()
        loads.append(copy)
        return copy

    small = []
    for side in range(2):
        x = side + odd - 2 * side * odd
        small.append(load(tentative.at[x], tent_v.at[side]))
        small.append(load(aggregate.at[x], agg_v.at[side]))
    big = []
    for side in range(2):
        x = side + odd - 2 * side * odd
        big.append(load(stencil.at[x], sten_v.at[side]))
        big.append(load(inverse.at[x], inv_v.at[side]))
        big.append(load(residual.at[x], res_v.at[side]))

    sends = []

    def send(src, dst, peer, leaves=None, arrives=None):
        at = len(sends)
        copy = pltpu.make_async_remote_copy(
            src_ref=src,
            dst_ref=dst,
            send_sem=send_sem.at[at],
            recv_sem=recv_sem.at[at],
            device_id=peer,
            device_id_type=MESH,
        )
        only(leaves, copy.start)
        sends.append((copy, leaves))
        return copy, arrives

    def await_all(copies):
        for copy, arrives in copies:
            only(arrives, copy.wait_recv)

    to_outer, to_outer2 = (has_outer, has_outer), (has_outer, has_back)
    to_below, to_above = (has_below, has_above), (has_above, has_below)

    @pl.when(jnp.logical_not(has_outer))
    def _():
        hx_v[0] = jnp.zeros(hx_v.shape[1:], BF16)
        hd_v[:, 0] = jnp.zeros((2, 16, 128), BF16)
        hkx_v[0] = jnp.zeros((6, 64, 128), BF16)
        hp0x_v[0] = jnp.zeros((4, 64, 128), BF16)
        rcv_v[4:7] = jnp.zeros((3, 64, 128), BF16)

    @pl.when(jnp.logical_not(has_back))
    def _():
        rcv_v[7] = jnp.zeros((64, 128), BF16)

    for end, condition in enumerate((has_below, has_above)):

        @pl.when(jnp.logical_not(condition))
        def _(end=end):
            hy_v[end] = jnp.zeros((2, 16, 128), BF16)
            hd_v[end] = jnp.zeros((2, 16, 128), BF16)
            hky_v[end] = jnp.zeros((2, 2, 64, 128), BF16)
            hp0y_v[end] = jnp.zeros((2, 64, 128), BF16)
            rcy_v[end] = jnp.zeros((4, 32, 128), BF16)

    lane = lax.broadcasted_iota(jnp.int32, (8, 128), 1)
    def packed(modes, code_0, code_1):
        code = jnp.where(
            lane < 64, jnp.broadcast_to(code_0, (8, 128)), jnp.broadcast_to(code_1, (8, 128))
        )
        return jnp.concatenate([modes.astype(F32), code.astype(F32)], axis=0).astype(BF16)

    for copy in small:
        copy.wait()

    own = {}
    for y in range(4):
        row = pl.ds(y, 1)
        tiles = []
        for side in range(2):
            tile = packed(tent_v[side, y], agg_v[side, 0:1, row], agg_v[side, 1:2, row])
            pack_v[side, y] = tile
            tiles.append(tile)
        own[y] = jnp.concatenate(tiles, axis=1).astype(F32)
        st_v[y] = expand(own[y])

    for copy in big:
        copy.wait()
    wide = lax.broadcasted_iota(jnp.int32, (64, 128), 1)
    low = wide < 64
    zero = jnp.zeros((64, 128), F32)

    def put(kind, y, place, first, second):
        rows = pl.ds(place * 64, 64)
        w_v[y, kind, rows, 0:128] = first.astype(BF16)
        w_v[y, kind, rows, 128:256] = second.astype(BF16)

    for y in range(4):
        for side in range(2):
            inv = inv_v[side, y].astype(F32)
            for z in range(2):
                place = 2 * side + z
                block = jnp.where(low if z == 0 else jnp.logical_not(low), inv, 0.0)
                tiles = [block, zero] if side == 0 else [zero, block]
                wb_v[y, pl.ds(place * 64, 64), 0:128] = tiles[0].astype(BF16)
                wb_v[y, pl.ds(place * 64, 64), 128:256] = tiles[1].astype(BF16)

                a = sten_v[side, y, z, :, 0:128].astype(F32)
                b = sten_v[side, y, z, :, 128:256].astype(F32)
                c = sten_v[side, y, z, :, 256:384].astype(F32)
                d = sten_v[side, y, z, :, 384:448].astype(F32)
                d = jnp.concatenate([d, d], axis=1)
                ra, rb, rc = swap(a), swap(b), swap(c)
                if z == 0:
                    centre = jnp.where(low, a, d)
                    toward_o, toward_i = jnp.where(is_odd, b, ra), jnp.where(is_odd, ra, b)
                    toward_m, toward_p = rb, c
                    keep = low
                else:
                    centre = jnp.where(low, rc, ra)
                    toward_o, toward_i = jnp.where(is_odd, rb, a), jnp.where(is_odd, a, rb)
                    toward_m, toward_p = b, rc
                    keep = jnp.logical_not(low)
                toward_o = jnp.where(keep, toward_o, 0.0)
                toward_i = jnp.where(keep, toward_i, 0.0)
                toward_m = jnp.where(keep, toward_m, 0.0)
                toward_p = jnp.where(keep, toward_p, 0.0)
                if side == 0:
                    put(0, y, place, centre, toward_i)
                    put(1, y, place, toward_o, zero)
                    put(2, y, place, toward_m, zero)
                    put(3, y, place, toward_p, zero)
                else:
                    put(0, y, place, toward_o, centre)
                    put(1, y, place, zero, toward_i)
                    put(2, y, place, zero, toward_m)
                    put(3, y, place, zero, toward_p)

    for y in range(4):
        blocks = jnp.concatenate([inv_v[0, y], inv_v[1, y]], axis=1)
        put_halves(k_v, X_AT[y], nn(blocks, w_v[y, 1]))
        if y in Y_AT:
            put_halves(k_v, Y_AT[y], nn(blocks, w_v[y, 2 if y == 0 else 3]))

    pl.semaphore_wait(barrier, awaited)
    corner_above = (jnp.logical_and(has_outer, has_above), jnp.logical_and(has_outer, has_below))
    corner_below = (corner_above[1], corner_above[0])
    seeds = [
        send(pack_v.at[:, 3], hy_v.at[0], (gx, above), *to_above),
        send(pack_v.at[:, 0], hy_v.at[1], (gx, below), *to_below),
        send(pack_v.at[0], hx_v.at[0], (outer, gy), *to_outer),
        send(pack_v.at[1], hx_v.at[1], (partner, gy)),
    ]
    corner_seeds = [
        send(pack_v.at[0, 3], hd_v.at[0, 0], (outer, above), *corner_above),
        send(pack_v.at[1, 3], hd_v.at[0, 1], (partner, above), *to_above),
        send(pack_v.at[0, 0], hd_v.at[1, 0], (outer, below), *corner_below),
        send(pack_v.at[1, 0], hd_v.at[1, 1], (partner, below), *to_below),
    ]
    products = [
        send(k_v.at[:, 4:6], hky_v.at[0], (gx, above), *to_above),
        send(k_v.at[:, 0:2], hky_v.at[1], (gx, below), *to_below),
        send(k_v.at[0], hkx_v.at[0], (outer, gy), *to_outer),
        send(k_v.at[1], hkx_v.at[1], (partner, gy)),
    ]

    applied = {}
    for y in (3, 0, 1, 2):
        total = nt(st_v[y], w_v[y, 0])
        if y > 0:
            total = total + nt(st_v[y - 1], w_v[y, 2])
        if y < 3:
            total = total + nt(st_v[y + 1], w_v[y, 3])
        applied[y] = total.astype(BF16)
    for y in (3, 0, 1, 2):
        relaxed = nt(applied[y], wb_v[y])
        put_halves(p0_v, y, st_v[y].astype(F32) - RELAX * relaxed)
    first = [
        send(p0_v.at[:, 3], hp0y_v.at[0], (gx, above), *to_above),
        send(p0_v.at[:, 0], hp0y_v.at[1], (gx, below), *to_below),
        send(p0_v.at[0], hp0x_v.at[0], (outer, gy), *to_outer),
        send(p0_v.at[1], hp0x_v.at[1], (partner, gy)),
    ]

    out[...] = jnp.zeros(out.shape, F32)
    seeds_by = {y: by_element(own[y][0:MODES]) for y in range(4)}
    blank = jnp.zeros((64, 128), BF16)

    await_all(seeds)
    halos, corners = {}, {}
    for end, y in ((1, 3), (0, 0)):
        halos[Y_AT[y]] = jnp.concatenate([hy_v[end, 0], hy_v[end, 1]], axis=1).astype(F32)
    for y in range(4):
        halos[X_AT[y]] = jnp.concatenate([hx_v[0, y], hx_v[1, y]], axis=1).astype(F32)
    values = {at: slot_values(by_element(halos[at][0:MODES]), halves(k_v, at)) for at in halos}
    full = {at: spread_columns(values[at], halos[at][MODES:]) for at in halos}
    ly = {y: by_element(values[Y_AT[y]]) for y in Y_AT}
    for y in range(4):
        slot = full[X_AT[y]]
        lx_v[y, 0:64, 0:128] = slot[:, 0:128]
        lx_v[y, 0:64, 128:256] = blank
        lx_v[y, 64:128, 0:128] = blank
        lx_v[y, 64:128, 128:256] = slot[:, 128:256]
        if y in Y_AT:
            lx_v[y, 128:192] = full[Y_AT[y]]

    def left(y, rows):
        return jnp.concatenate([halves(p0_v, y), lx_v[y, 0 : rows - 64]], axis=0)

    terms = [jnp.zeros((rows, 1), F32) for rows in (64, 64, 64, 32, 32)]
    for y in range(4):
        res = jnp.concatenate([res_v[0, y : y + 1, :], res_v[1, y : y + 1, :]], axis=1)
        blocks = [(0, halves(p0_v, y)), (1, lx_v[y, 0:64]), (2, lx_v[y, 64:128])]
        if y in Y_AT:
            blocks.append((3 if y == 0 else 4, ly[y]))
        for slot, block in blocks:
            terms[slot] = terms[slot] + jnp.sum(block.astype(F32) * res, axis=1, keepdims=True)

    for y in range(4):
        size = 256 if y in Y_AT else 192
        acc_v[y, 0:size] = nt(left(y, size), w_v[y, 0])
        if y not in Y_AT:
            acc_v[y, 192:256] = jnp.zeros((64, 256), F32)
        if y > 0:
            size = 256 if y - 1 in Y_AT else 192
            acc_v[y, 0:size] = acc_v[y, 0:size] + nt(left(y - 1, size), w_v[y, 2])
        if y < 3:
            size = 256 if y + 1 in Y_AT else 192
            acc_v[y, 0:size] = acc_v[y, 0:size] + nt(left(y + 1, size), w_v[y, 3])

    await_all(corner_seeds)
    for end, y in ((1, 3), (0, 0)):
        corners[y] = jnp.concatenate([hd_v[end, 0], hd_v[end, 1]], axis=1).astype(F32)
    corners_by = {y: by_element(corners[y][0:MODES]) for y in Y_AT}
    await_all(products)
    near_x, near_y, far_x, far_y = {}, {}, {}, {}
    for y in (3, 0, 1, 2):
        near_x[y] = slot_values(seeds_by[y], halves(hkx_v, X_AT[y]))
    for end, y in ((1, 3), (0, 0)):
        near_y[y] = slot_values(seeds_by[y], halves(hky_v.at[end], 1))
        far_x[y] = slot_values(corners_by[y], halves(hkx_v, Y_AT[y]))
        far_y[y] = slot_values(corners_by[y], halves(hky_v.at[end], 0))
    near_x = {y: spread_columns(near_x[y], own[y][MODES:]) for y in range(4)}
    near_y = {y: spread_columns(near_y[y], own[y][MODES:]) for y in Y_AT}
    far_x = {y: spread_columns(far_x[y], corners[y][MODES:]) for y in Y_AT}
    far_y = {y: spread_columns(far_y[y], corners[y][MODES:]) for y in Y_AT}

    await_all(first)

    def coupled(y):
        rows = [halves(hp0x_v, y), near_x[y]] + ([far_x[y]] if y in Y_AT else [])
        part = nt(jnp.concatenate(rows, axis=0), w_v[y, 1])
        row_0 = acc_v[y, 0:64] + part[64:128]
        row_o, row_i, row_y = acc_v[y, 64:128], acc_v[y, 128:192], acc_v[y, 192:256]
        row_o = jnp.concatenate([row_o[:, 0:128] + part[0:64, 0:128], row_o[:, 128:256]], axis=1)
        row_i = jnp.concatenate([row_i[:, 0:128], row_i[:, 128:256] + part[0:64, 128:256]], axis=1)
        row_o, row_i = row_o.astype(BF16), row_i.astype(BF16)
        if y not in Y_AT:
            rows = [row_0.astype(BF16), row_y.astype(BF16), row_i, row_o]
            return jnp.concatenate(rows, axis=0)
        end = 0 if y == 0 else 1
        rows = [halves(hp0y_v, end, 1), far_y[y], near_y[y]]
        more = nt(jnp.concatenate(rows, axis=0), w_v[y, 2 + end])
        row_0, row_y = (row_0 + more[128:192]).astype(BF16), (row_y + more[0:64]).astype(BF16)
        corner = (part[128:192] + more[64:128]).astype(BF16)
        corner_o = jnp.concatenate([corner[:, 0:128], blank], axis=1)
        corner_i = jnp.concatenate([blank, corner[:, 128:256]], axis=1)
        return jnp.concatenate([row_0, row_y, corner_o, row_o, corner_i, row_i], axis=0)

    right = {y: coupled(y) for y in (3, 0, 1, 2)}
    g3 = nt(jnp.concatenate([left(3, 192), ly[3]], axis=0), right[3])
    g0 = nt(jnp.concatenate([left(0, 192), ly[0]], axis=0), right[0])
    g1 = nt(left(1, 192), right[1])
    g2 = nt(left(2, 192), right[2])

    def pick(first, second):
        shape = first.shape if hasattr(first, "shape") else second.shape
        return jnp.where(wide[0 : shape[0]] < 64, first, second)

    def half(tile, near):
        moved = pick(tile, pltpu.roll(tile, 96, 1))
        return jnp.where(is_odd, moved, tile) if near else jnp.where(is_odd, tile, moved)

    def with_terms(tile, term):
        upper = term.astype(BF16).astype(F32)
        at = wide[0 : tile.shape[0]]
        return jnp.where(at == 96, upper, jnp.where(at == 97, term - upper, tile))

    def with_codes(tile, y):
        code = halos[Y_AT[y]][MODES:]
        cells = [code[:, 64 * e : 64 * e + 1] for e in range(4)]
        column = jnp.concatenate(
            [jnp.broadcast_to(cell, (MODES, 128)) for cell in cells], axis=0
        )
        return jnp.where(wide[0:32] == 112, column, tile)

    def tiles(product, slot):
        rows = product[slot * 64 : slot * 64 + 64]
        return [rows[:, 128 * t : 128 * t + 128] for t in range(rows.shape[1] // 128)]

    def post(at, values):
        for n, value in enumerate(values):
            snd_v[at + n] = value.astype(BF16)

    msgs = []
    for end, g, y, peer, way in ((1, g3, 3, above, to_above), (0, g0, 0, below, to_below)):
        t0, t1, t2 = [g[192:224, 128 * t : 128 * t + 128] for t in range(3)]
        kept = (jnp.where(is_odd, 0.0, t0), t0) if end else (jnp.where(is_odd, t0, 0.0), t0)
        near = half(pick(*kept), True)
        kept = (jnp.where(is_odd, t0, 0.0), t0) if end else (jnp.where(is_odd, 0.0, t0), t0)
        far = half(pick(*kept), False)
        sny_v[end, 0] = with_codes(with_terms(near, terms[3 + end]), y).astype(BF16)
        sny_v[end, 1] = t1.astype(BF16)
        sny_v[end, 2] = with_codes(far, y).astype(BF16)
        sny_v[end, 3] = t2.astype(BF16)
        msgs += [
            send(sny_v.at[end, 0:2], rcy_v.at[1 - end, 0:2], (gx, peer), *way),
            send(sny_v.at[end, 2:4], rcy_v.at[1 - end, 2:4], (partner, peer), *way),
        ]

    def summed(slot):
        a0, a1, a2 = tiles(g0, slot)
        b0, b1, b2 = tiles(g3, slot)
        c0, c1 = tiles(g1, slot)
        d0, d1 = tiles(g2, slot)
        um, up = a0 + c0, b0 + d0
        mid = c1 + d1
        return um, up, um + up, a1, b1, a1 + b1 + mid, a2, b2, a2 + b2 + swap(mid)

    def by_side(first, second):
        return jnp.where(is_odd, second, first)

    um, up, mid, om, op, o_sum, im, ip, i_sum = summed(1)
    post(
        4,
        [
            with_terms(half(pick(by_side(op, om), o_sum), False), terms[1]),
            pick(mid, up),
            pick(swap(um), i_sum),
        ],
    )
    post(7, [half(pick(by_side(om, op), o_sum), True)])
    msgs += [
        send(snd_v.at[4:7], rcv_v.at[4:7], (outer, gy), *to_outer),
        send(snd_v.at[7:8], rcv_v.at[7:8], (outer2, gy), *to_outer2),
    ]
    um, up, mid, om, op, o_sum, im, ip, i_sum = summed(2)
    post(3, [with_terms(half(pick(by_side(ip, im), i_sum), False), terms[2])])
    far_a = half(pick(by_side(im, ip), i_sum), True)
    far_b = pick(mid, up)
    far_c = pick(swap(um), o_sum)
    um, up, mid, om, op, o_sum, im, ip, i_sum = summed(0)
    post(
        0,
        [
            half(swap(pick(mid, by_side(up, um))), False),
            swap(pick(ip, i_sum)),
            pick(im, 0.0),
        ],
    )
    msgs += [send(snd_v.at[0:4], rcv_v.at[0:4], (partner, gy))]
    own_a = with_terms(half(swap(pick(mid, by_side(um, up))), True), terms[0])
    own_b = swap(pick(op, o_sum))
    own_c = pick(om, 0.0)

    def got(at):
        return rcv_v[at].astype(F32)

    def spread(end, at):
        first, second = rcy_v[end, at].astype(F32), rcy_v[end, at + 1].astype(F32)
        code = jnp.broadcast_to(first[:, 112:113], (32, 128))
        results = []
        for tile in (first, second):
            rows = []
            for a in range(AGG):
                here = jnp.where(code == float(a), tile, 0.0)
                rows.append(here[0:8] + here[8:16] + here[16:24] + here[24:32])
            results.append(jnp.concatenate(rows, axis=0))
        return results

    for copy, leaves in sends[: -len(msgs)]:
        only(leaves, copy.wait_send)

    await_all(msgs[6:7])
    own_a, far_a = own_a + got(3), far_a + got(0)
    far_b, far_c = far_b + got(1), far_c + got(2)
    await_all(msgs[2:4])
    (near_a, near_b), (past_a, past_b) = spread(1, 0), spread(1, 2)
    own_a, own_b = own_a + near_a, own_b + near_b
    far_a, far_b = far_a + past_a, far_b + past_b
    await_all(msgs[4:6])
    own_a, own_b, own_c = own_a + got(4), own_b + got(5), own_c + got(6)
    far_a = far_a + got(7)
    for copy, leaves in sends[-len(msgs) :]:
        only(leaves, copy.wait_send)
    await_all(msgs[0:2])
    (near_a, near_b), (past_a, past_b) = spread(0, 0), spread(0, 2)
    own_a, own_b = own_a + near_a, own_b + pick(near_b, 0.0)
    own_c = own_c + pick(swap(near_b), 0.0)
    far_a, far_b = far_a + past_a, far_b + pick(past_b, 0.0)
    far_c = far_c + pick(swap(past_b), 0.0)

    def both(own, far):
        first, second = jnp.where(is_odd, far, own), jnp.where(is_odd, own, far)
        return jnp.concatenate([first, second], axis=0).T

    a, b, c = both(own_a, far_a), both(own_b, far_b), both(own_c, far_c)

    @pl.when(odd == 0)
    def _():
        out[128:192] = c[64:128]
        out[320:384] = c[0:64]
        out[384:512] = b
        out[704:800] = a[0:96]
        out[800:801] = a[96:97] + a[97:98]

    @pl.when(odd == 1)
    def _():
        out[0:32] = a[64:96]
        out[32:96] = a[0:64]
        out[288:352] = c[0:64]
        out[352:480] = b
        out[608:672] = c[64:128]
        out[800:801] = swap(a[96:97] + a[97:98])


def finish_kernel(data, coarse, restricted, row, sem):
    first = pltpu.make_async_copy(data.at[pl.ds(0, 800)], coarse.at[0, 0], sem.at[0])
    first.start()
    row[...] = data[800:801, 0:64]
    second = pltpu.make_async_copy(row, restricted.at[0], sem.at[1])
    second.start()
    first.wait()
    second.wait()


def body(stencil, inverse, tentative, aggregate, residual):
    hbm = pl.BlockSpec(memory_space=pltpu.HBM)
    aggregate = aggregate.transpose(0, 2, 1)
    operands = [
        pltpu.with_memory_space_constraint(operand, pltpu.HBM)
        for operand in (stencil, inverse, tentative, aggregate, residual)
    ]
    vmem = pl.BlockSpec(memory_space=pltpu.VMEM)
    scratch = [
        pltpu.VMEM(stencil.shape, BF16),
        pltpu.VMEM(inverse.shape, BF16),
        pltpu.VMEM(tentative.shape, BF16),
        pltpu.VMEM(aggregate.shape, jnp.int32),
        pltpu.VMEM(residual.shape, F32),
        pltpu.VMEM((4, 4, 256, 256), BF16),
        pltpu.VMEM((4, 256, 256), BF16),
        pltpu.VMEM((2, 4, 16, 128), BF16),
        pltpu.VMEM((2, 4, 16, 128), BF16),
        pltpu.VMEM((2, 2, 16, 128), BF16),
        pltpu.VMEM((2, 2, 16, 128), BF16),
        pltpu.VMEM((2, 6, 64, 128), BF16),
        pltpu.VMEM((2, 6, 64, 128), BF16),
        pltpu.VMEM((2, 2, 2, 64, 128), BF16),
        pltpu.VMEM((2, 4, 64, 128), BF16),
        pltpu.VMEM((2, 4, 64, 128), BF16),
        pltpu.VMEM((2, 2, 64, 128), BF16),
        pltpu.VMEM((4, 64, 256), BF16),
        pltpu.VMEM((4, 192, 256), BF16),
        pltpu.VMEM((4, 256, 256), F32),
        pltpu.VMEM((8, 64, 128), BF16),
        pltpu.VMEM((8, 64, 128), BF16),
        pltpu.VMEM((2, 4, 32, 128), BF16),
        pltpu.VMEM((2, 4, 32, 128), BF16),
        pltpu.SemaphoreType.DMA((10,)),
        pltpu.SemaphoreType.DMA((23,)),
        pltpu.SemaphoreType.DMA((23,)),
    ]
    sizes = (lax.axis_size("gx"), lax.axis_size("gy"))

    def call(*refs):
        kernel(*sizes, *refs)

    coarse = pl.pallas_call(
        call,
        out_shape=pltpu.VMEM((808, 128), F32),
        in_specs=[hbm] * 5,
        out_specs=vmem,
        scratch_shapes=scratch,
        compiler_params=pltpu.CompilerParams(
            collective_id=0, has_side_effects=True, vmem_limit_bytes=32 << 20
        ),
        name="galerkin",
    )(*operands)
    coarse, restricted = pl.pallas_call(
        finish_kernel,
        out_shape=(
            jax.ShapeDtypeStruct((1, 1, 800, 128), F32),
            jax.ShapeDtypeStruct((1, 1, 64), F32),
        ),
        in_specs=[pl.BlockSpec(memory_space=pltpu.VMEM)],
        out_specs=(pl.BlockSpec(memory_space=pl.ANY), pl.BlockSpec(memory_space=pl.ANY)),
        scratch_shapes=[pltpu.VMEM((1, 64), F32), pltpu.SemaphoreType.DMA((2,))],
        name="store",
    )(pltpu.with_memory_space_constraint(coarse, pltpu.VMEM))
    return coarse.swapaxes(2, 3), restricted


def solution(mesh):
    in_specs = (
        P("gx", "gy", None, None, None),
        P("gx", "gy", None, None),
        P("gx", "gy", None, None),
        P("gx", "gy", None),
        P("gx", "gy", None),
    )
    out_specs = (P("gx", "gy", None, None), P("gx", "gy", None))
    return jax.shard_map(body, mesh=mesh, in_specs=in_specs, out_specs=out_specs, check_vma=False)
```

```python
import jax
import jax.numpy as jnp
from jax import lax
from jax.experimental import pallas as pl
from jax.experimental.pallas import tpu as pltpu
from jax.sharding import PartitionSpec as P

MESH = pl.DeviceIdType.MESH
F32, BF16 = jnp.float32, jnp.bfloat16
AGG = 8
MODES = 8
RELAX = 0.6


X_AT, Y_AT = (0, 2, 3, 4), {0: 1, 3: 5}


def nt(left, right):
    return lax.dot_general(left, right, (((1,), (1,)), ((), ())), preferred_element_type=F32)


def nn(left, right):
    return lax.dot_general(left, right, (((1,), (0,)), ((), ())), preferred_element_type=F32)


def spread_columns(values, code):
    rows = [jnp.where(code == float(a), values, 0.0) for a in range(AGG)]
    return jnp.concatenate(rows, axis=0).astype(BF16)


def expand(tile):
    return spread_columns(tile[0:MODES].astype(F32), tile[MODES : 2 * MODES].astype(F32))


def by_element(values):
    lane = lax.broadcasted_iota(jnp.int32, (MODES, 256), 1)
    parts = [
        jnp.where(jnp.logical_and(lane >= 64 * e, lane < 64 * e + 64), values, 0.0)
        for e in range(4)
    ]
    return jnp.concatenate(parts, axis=0).astype(BF16)


def slot_values(seeds, product):
    rows = -RELAX * nt(seeds, product)
    values = jnp.concatenate([rows[8 * e : 8 * e + 8] for e in range(4)], axis=1)
    return values.astype(BF16).astype(F32)


def swap(tile):
    return pltpu.roll(tile, 64, 1)


def kernel(
    n_gx,
    n_gy,
    stencil,
    inverse,
    tentative,
    aggregate,
    residual,
    out,
    sten_v,
    inv_v,
    tent_v,
    agg_v,
    res_v,
    w_v,
    wb_v,
    pack_v,
    hx_v,
    hy_v,
    hd_v,
    k_v,
    hkx_v,
    hky_v,
    p0_v,
    hp0x_v,
    hp0y_v,
    st_v,
    lx_v,
    acc_v,
    snd_v,
    rcv_v,
    sny_v,
    rcy_v,
    load_sem,
    send_sem,
    recv_sem,
):
    gx, gy = lax.axis_index("gx"), lax.axis_index("gy")
    odd = lax.rem(gx, 2)
    is_odd = odd == 1
    turn = 2 * odd - 1
    partner = gx - turn
    outer = lax.rem(gx + turn + n_gx, n_gx)
    outer2 = lax.rem(gx + 2 * turn + n_gx, n_gx)
    back2 = lax.rem(gx - 2 * turn + n_gx, n_gx)
    below = lax.rem(gy - 1 + n_gy, n_gy)
    above = lax.rem(gy + 1, n_gy)
    has_outer = jnp.logical_and(gx > 0, gx < n_gx - 1)
    has_back = jnp.logical_and(partner > 0, partner < n_gx - 1)
    has_below, has_above = gy > 0, gy < n_gy - 1

    def only(condition, action):
        if condition is None:
            action()
        else:
            pl.when(condition)(action)

    barrier = pltpu.get_barrier_semaphore()
    peers = [
        ((gx, above), has_above),
        ((partner, above), has_above),
        ((outer, above), jnp.logical_and(has_outer, has_above)),
        ((gx, below), has_below),
        ((partner, below), has_below),
        ((outer, below), jnp.logical_and(has_outer, has_below)),
        ((outer, gy), has_outer),
        ((outer2, gy), has_outer),
        ((back2, gy), has_back),
        ((partner, gy), None),
    ]
    for peer, condition in peers:
        only(
            condition,
            lambda peer=peer: pl.semaphore_signal(
                barrier, inc=1, device_id=peer, device_id_type=MESH
            ),
        )
    awaited = 1
    for _, condition in peers[:-1]:
        awaited = awaited + jnp.where(condition, 1, 0)

    loads = []

    def load(src, dst):
        copy = pltpu.make_async_copy(src, dst, load_sem.at[len(loads)])
        copy.start()
        loads.append(copy)
        return copy

    small = []
    for side in range(2):
        x = side + odd - 2 * side * odd
        small.append(load(tentative.at[x], tent_v.at[side]))
        small.append(load(aggregate.at[x], agg_v.at[side]))
    big = []
    for side in range(2):
        x = side + odd - 2 * side * odd
        big.append(load(stencil.at[x], sten_v.at[side]))
        big.append(load(inverse.at[x], inv_v.at[side]))
        big.append(load(residual.at[x], res_v.at[side]))

    sends, pending = [], []

    def send(src, dst, peer, leaves=None, arrives=None):
        at = len(sends)
        copy = pltpu.make_async_remote_copy(
            src_ref=src,
            dst_ref=dst,
            send_sem=send_sem.at[at],
            recv_sem=recv_sem.at[at],
            device_id=peer,
            device_id_type=MESH,
        )
        sends.append((copy, leaves))
        pending.append((copy, leaves))
        return copy, arrives

    def together(copies, act):
        groups = {}
        for copy, condition in copies:
            groups.setdefault(id(condition), (condition, []))[1].append(copy)
        for condition, group in groups.values():
            only(condition, lambda group=group: [act(copy) for copy in group] and None)

    def launch():
        together(pending, lambda copy: copy.start())
        pending.clear()

    def await_all(copies):
        together(copies, lambda copy: copy.wait_recv())

    to_outer, to_outer2 = (has_outer, has_outer), (has_outer, has_back)
    to_below, to_above = (has_below, has_above), (has_above, has_below)

    @pl.when(jnp.logical_not(has_outer))
    def _():
        hx_v[0] = jnp.zeros(hx_v.shape[1:], BF16)
        hd_v[:, 0] = jnp.zeros((2, 16, 128), BF16)
        hkx_v[:, :, 0:128] = jnp.zeros((6, 64, 128), BF16)
        hp0x_v[:, :, 0:128] = jnp.zeros((4, 64, 128), BF16)
        rcv_v[4:7] = jnp.zeros((3, 64, 128), BF16)

    @pl.when(jnp.logical_not(has_back))
    def _():
        rcv_v[7] = jnp.zeros((64, 128), BF16)

    for end, condition in enumerate((has_below, has_above)):

        @pl.when(jnp.logical_not(condition))
        def _(end=end):
            hy_v[end] = jnp.zeros((2, 16, 128), BF16)
            hd_v[end] = jnp.zeros((2, 16, 128), BF16)
            hky_v[end] = jnp.zeros((2, 64, 256), BF16)
            hp0y_v[end] = jnp.zeros((64, 256), BF16)
            rcy_v[end] = jnp.zeros((4, 32, 128), BF16)

    lane = lax.broadcasted_iota(jnp.int32, (8, 128), 1)
    def packed(modes, code_0, code_1):
        code = jnp.where(
            lane < 64, jnp.broadcast_to(code_0, (8, 128)), jnp.broadcast_to(code_1, (8, 128))
        )
        return jnp.concatenate([modes.astype(F32), code.astype(F32)], axis=0).astype(BF16)

    for copy in small:
        copy.wait()

    own = {}
    for y in range(4):
        row = pl.ds(y, 1)
        tiles = []
        for side in range(2):
            tile = packed(tent_v[side, y], agg_v[side, 0:1, row], agg_v[side, 1:2, row])
            pack_v[side, y] = tile
            tiles.append(tile)
        own[y] = jnp.concatenate(tiles, axis=1).astype(F32)
        st_v[y] = expand(own[y])

    for copy in big:
        copy.wait()
    wide = lax.broadcasted_iota(jnp.int32, (64, 128), 1)
    low = wide < 64
    zero = jnp.zeros((64, 128), F32)

    def put(kind, y, place, first, second):
        rows = pl.ds(place * 64, 64)
        w_v[y, kind, rows, 0:128] = first.astype(BF16)
        w_v[y, kind, rows, 128:256] = second.astype(BF16)

    for y in range(4):
        for side in range(2):
            inv = inv_v[side, y].astype(F32)
            for z in range(2):
                place = 2 * side + z
                block = jnp.where(low if z == 0 else jnp.logical_not(low), inv, 0.0)
                tiles = [block, zero] if side == 0 else [zero, block]
                wb_v[y, pl.ds(place * 64, 64), 0:128] = tiles[0].astype(BF16)
                wb_v[y, pl.ds(place * 64, 64), 128:256] = tiles[1].astype(BF16)

                a = sten_v[side, y, z, :, 0:128].astype(F32)
                b = sten_v[side, y, z, :, 128:256].astype(F32)
                c = sten_v[side, y, z, :, 256:384].astype(F32)
                d = sten_v[side, y, z, :, 384:448].astype(F32)
                d = jnp.concatenate([d, d], axis=1)
                ra, rb, rc = swap(a), swap(b), swap(c)
                if z == 0:
                    centre = jnp.where(low, a, d)
                    toward_o, toward_i = jnp.where(is_odd, b, ra), jnp.where(is_odd, ra, b)
                    toward_m, toward_p = rb, c
                    keep = low
                else:
                    centre = jnp.where(low, rc, ra)
                    toward_o, toward_i = jnp.where(is_odd, rb, a), jnp.where(is_odd, a, rb)
                    toward_m, toward_p = b, rc
                    keep = jnp.logical_not(low)
                toward_o = jnp.where(keep, toward_o, 0.0)
                toward_i = jnp.where(keep, toward_i, 0.0)
                toward_m = jnp.where(keep, toward_m, 0.0)
                toward_p = jnp.where(keep, toward_p, 0.0)
                if side == 0:
                    put(0, y, place, centre, toward_i)
                    put(1, y, place, toward_o, zero)
                    put(2, y, place, toward_m, zero)
                    put(3, y, place, toward_p, zero)
                else:
                    put(0, y, place, toward_o, centre)
                    put(1, y, place, zero, toward_i)
                    put(2, y, place, zero, toward_m)
                    put(3, y, place, zero, toward_p)

    for y in range(4):
        blocks = jnp.concatenate([inv_v[0, y], inv_v[1, y]], axis=1)
        k_v[X_AT[y]] = nn(blocks, w_v[y, 1]).astype(BF16)
        if y in Y_AT:
            k_v[Y_AT[y]] = nn(blocks, w_v[y, 2 if y == 0 else 3]).astype(BF16)

    applied = {}
    for y in (3, 0, 1, 2):
        total = nt(st_v[y], w_v[y, 0])
        if y > 0:
            total = total + nt(st_v[y - 1], w_v[y, 2])
        if y < 3:
            total = total + nt(st_v[y + 1], w_v[y, 3])
        applied[y] = total.astype(BF16)
    for y in (3, 0, 1, 2):
        relaxed = nt(applied[y], wb_v[y])
        p0_v[y] = (st_v[y].astype(F32) - RELAX * relaxed).astype(BF16)
    pl.semaphore_wait(barrier, awaited)
    corner_above = (jnp.logical_and(has_outer, has_above), jnp.logical_and(has_outer, has_below))
    corner_below = (corner_above[1], corner_above[0])
    seeds = [
        send(pack_v.at[:, 3], hy_v.at[0], (gx, above), *to_above),
        send(pack_v.at[0, 3], hd_v.at[0, 0], (outer, above), *corner_above),
        send(pack_v.at[1, 3], hd_v.at[0, 1], (partner, above), *to_above),
        send(pack_v.at[:, 0], hy_v.at[1], (gx, below), *to_below),
        send(pack_v.at[0, 0], hd_v.at[1, 0], (outer, below), *corner_below),
        send(pack_v.at[1, 0], hd_v.at[1, 1], (partner, below), *to_below),
        send(pack_v.at[0], hx_v.at[0], (outer, gy), *to_outer),
        send(pack_v.at[1], hx_v.at[1], (partner, gy)),
    ]
    products = [
        send(k_v.at[4:6], hky_v.at[0], (gx, above), *to_above),
        send(k_v.at[0:2], hky_v.at[1], (gx, below), *to_below),
        send(k_v.at[:, :, 0:128], hkx_v.at[:, :, 0:128], (outer, gy), *to_outer),
        send(k_v.at[:, :, 128:256], hkx_v.at[:, :, 128:256], (partner, gy)),
    ]

    first = [
        send(p0_v.at[3], hp0y_v.at[0], (gx, above), *to_above),
        send(p0_v.at[0], hp0y_v.at[1], (gx, below), *to_below),
        send(p0_v.at[:, :, 0:128], hp0x_v.at[:, :, 0:128], (outer, gy), *to_outer),
        send(p0_v.at[:, :, 128:256], hp0x_v.at[:, :, 128:256], (partner, gy)),
    ]

    launch()
    out[...] = jnp.zeros(out.shape, F32)
    seeds_by = {y: by_element(own[y][0:MODES]) for y in range(4)}
    blank = jnp.zeros((64, 128), BF16)

    await_all(seeds)
    halos, corners = {}, {}
    for end, y in ((1, 3), (0, 0)):
        halos[Y_AT[y]] = jnp.concatenate([hy_v[end, 0], hy_v[end, 1]], axis=1).astype(F32)
        corners[y] = jnp.concatenate([hd_v[end, 0], hd_v[end, 1]], axis=1).astype(F32)
    for y in range(4):
        halos[X_AT[y]] = jnp.concatenate([hx_v[0, y], hx_v[1, y]], axis=1).astype(F32)
    values = {at: slot_values(by_element(halos[at][0:MODES]), k_v[at]) for at in halos}
    full = {at: spread_columns(values[at], halos[at][MODES:]) for at in halos}
    corners_by = {y: by_element(corners[y][0:MODES]) for y in Y_AT}
    ly = {y: by_element(values[Y_AT[y]]) for y in Y_AT}
    for y in range(4):
        slot = full[X_AT[y]]
        lx_v[y, 0:64, 0:128] = slot[:, 0:128]
        lx_v[y, 0:64, 128:256] = blank
        lx_v[y, 64:128, 0:128] = blank
        lx_v[y, 64:128, 128:256] = slot[:, 128:256]
        if y in Y_AT:
            lx_v[y, 128:192] = full[Y_AT[y]]

    def left(y, rows):
        return jnp.concatenate([p0_v[y], lx_v[y, 0 : rows - 64]], axis=0)

    terms = [jnp.zeros((rows, 1), F32) for rows in (64, 64, 64, 32, 32)]
    for y in range(4):
        res = jnp.concatenate([res_v[0, y : y + 1, :], res_v[1, y : y + 1, :]], axis=1)
        blocks = [(0, p0_v[y]), (1, lx_v[y, 0:64]), (2, lx_v[y, 64:128])]
        if y in Y_AT:
            blocks.append((3 if y == 0 else 4, ly[y]))
        for slot, block in blocks:
            terms[slot] = terms[slot] + jnp.sum(block.astype(F32) * res, axis=1, keepdims=True)

    for y in range(4):
        size = 256 if y in Y_AT else 192
        acc_v[y, 0:size] = nt(left(y, size), w_v[y, 0])
        if y not in Y_AT:
            acc_v[y, 192:256] = jnp.zeros((64, 256), F32)
        if y > 0:
            size = 256 if y - 1 in Y_AT else 192
            acc_v[y, 0:size] = acc_v[y, 0:size] + nt(left(y - 1, size), w_v[y, 2])
        if y < 3:
            size = 256 if y + 1 in Y_AT else 192
            acc_v[y, 0:size] = acc_v[y, 0:size] + nt(left(y + 1, size), w_v[y, 3])

    await_all(products)
    near_x, near_y, far_x, far_y = {}, {}, {}, {}
    for y in (3, 0, 1, 2):
        near_x[y] = slot_values(seeds_by[y], hkx_v[X_AT[y]])
    for end, y in ((1, 3), (0, 0)):
        near_y[y] = slot_values(seeds_by[y], hky_v[end, 1])
        far_x[y] = slot_values(corners_by[y], hkx_v[Y_AT[y]])
        far_y[y] = slot_values(corners_by[y], hky_v[end, 0])
    near_x = {y: spread_columns(near_x[y], own[y][MODES:]) for y in range(4)}
    near_y = {y: spread_columns(near_y[y], own[y][MODES:]) for y in Y_AT}
    far_x = {y: spread_columns(far_x[y], corners[y][MODES:]) for y in Y_AT}
    far_y = {y: spread_columns(far_y[y], corners[y][MODES:]) for y in Y_AT}

    await_all(first)

    def coupled(y):
        rows = [hp0x_v[y], near_x[y]] + ([far_x[y]] if y in Y_AT else [])
        part = nt(jnp.concatenate(rows, axis=0), w_v[y, 1])
        row_0 = acc_v[y, 0:64] + part[64:128]
        row_o, row_i, row_y = acc_v[y, 64:128], acc_v[y, 128:192], acc_v[y, 192:256]
        row_o = jnp.concatenate([row_o[:, 0:128] + part[0:64, 0:128], row_o[:, 128:256]], axis=1)
        row_i = jnp.concatenate([row_i[:, 0:128], row_i[:, 128:256] + part[0:64, 128:256]], axis=1)
        row_o, row_i = row_o.astype(BF16), row_i.astype(BF16)
        if y not in Y_AT:
            rows = [row_0.astype(BF16), row_y.astype(BF16), row_i, row_o]
            return jnp.concatenate(rows, axis=0)
        end = 0 if y == 0 else 1
        rows = [hp0y_v[end], far_y[y], near_y[y]]
        more = nt(jnp.concatenate(rows, axis=0), w_v[y, 2 + end])
        row_0, row_y = (row_0 + more[128:192]).astype(BF16), (row_y + more[0:64]).astype(BF16)
        corner = (part[128:192] + more[64:128]).astype(BF16)
        corner_o = jnp.concatenate([corner[:, 0:128], blank], axis=1)
        corner_i = jnp.concatenate([blank, corner[:, 128:256]], axis=1)
        return jnp.concatenate([row_0, row_y, corner_o, row_o, corner_i, row_i], axis=0)

    right = {y: coupled(y) for y in (3, 0, 1, 2)}
    g3 = nt(jnp.concatenate([left(3, 192), ly[3]], axis=0), right[3])
    g0 = nt(jnp.concatenate([left(0, 192), ly[0]], axis=0), right[0])
    g1 = nt(left(1, 192), right[1])
    g2 = nt(left(2, 192), right[2])

    def pick(first, second):
        shape = first.shape if hasattr(first, "shape") else second.shape
        return jnp.where(wide[0 : shape[0]] < 64, first, second)

    def half(tile, near):
        moved = pick(tile, pltpu.roll(tile, 96, 1))
        return jnp.where(is_odd, moved, tile) if near else jnp.where(is_odd, tile, moved)

    def with_terms(tile, term):
        upper = term.astype(BF16).astype(F32)
        at = wide[0 : tile.shape[0]]
        return jnp.where(at == 96, upper, jnp.where(at == 97, term - upper, tile))

    def with_codes(tile, y):
        code = halos[Y_AT[y]][MODES:]
        cells = [code[:, 64 * e : 64 * e + 1] for e in range(4)]
        column = jnp.concatenate(
            [jnp.broadcast_to(cell, (MODES, 128)) for cell in cells], axis=0
        )
        return jnp.where(wide[0:32] == 112, column, tile)

    def tiles(product, slot):
        rows = product[slot * 64 : slot * 64 + 64]
        return [rows[:, 128 * t : 128 * t + 128] for t in range(rows.shape[1] // 128)]

    def post(at, values):
        for n, value in enumerate(values):
            snd_v[at + n] = value.astype(BF16)

    msgs = []
    for end, g, y, peer, way in ((1, g3, 3, above, to_above), (0, g0, 0, below, to_below)):
        t0, t1, t2 = [g[192:224, 128 * t : 128 * t + 128] for t in range(3)]
        kept = (jnp.where(is_odd, 0.0, t0), t0) if end else (jnp.where(is_odd, t0, 0.0), t0)
        near = half(pick(*kept), True)
        kept = (jnp.where(is_odd, t0, 0.0), t0) if end else (jnp.where(is_odd, 0.0, t0), t0)
        far = half(pick(*kept), False)
        sny_v[end, 0] = with_codes(with_terms(near, terms[3 + end]), y).astype(BF16)
        sny_v[end, 1] = t1.astype(BF16)
        sny_v[end, 2] = with_codes(far, y).astype(BF16)
        sny_v[end, 3] = t2.astype(BF16)
        msgs += [
            send(sny_v.at[end, 0:2], rcy_v.at[1 - end, 0:2], (gx, peer), *way),
            send(sny_v.at[end, 2:4], rcy_v.at[1 - end, 2:4], (partner, peer), *way),
        ]

    launch()

    def summed(slot):
        a0, a1, a2 = tiles(g0, slot)
        b0, b1, b2 = tiles(g3, slot)
        c0, c1 = tiles(g1, slot)
        d0, d1 = tiles(g2, slot)
        um, up = a0 + c0, b0 + d0
        mid = c1 + d1
        return um, up, um + up, a1, b1, a1 + b1 + mid, a2, b2, a2 + b2 + swap(mid)

    def by_side(first, second):
        return jnp.where(is_odd, second, first)

    um, up, mid, om, op, o_sum, im, ip, i_sum = summed(1)
    post(
        4,
        [
            with_terms(half(pick(by_side(op, om), o_sum), False), terms[1]),
            pick(mid, up),
            pick(swap(um), i_sum),
        ],
    )
    post(7, [half(pick(by_side(om, op), o_sum), True)])
    msgs += [
        send(snd_v.at[4:7], rcv_v.at[4:7], (outer, gy), *to_outer),
        send(snd_v.at[7:8], rcv_v.at[7:8], (outer2, gy), *to_outer2),
    ]
    launch()
    um, up, mid, om, op, o_sum, im, ip, i_sum = summed(2)
    post(3, [with_terms(half(pick(by_side(ip, im), i_sum), False), terms[2])])
    far_a = half(pick(by_side(im, ip), i_sum), True)
    far_b = pick(mid, up)
    far_c = pick(swap(um), o_sum)
    um, up, mid, om, op, o_sum, im, ip, i_sum = summed(0)
    post(
        0,
        [
            half(swap(pick(mid, by_side(up, um))), False),
            swap(pick(ip, i_sum)),
            pick(im, 0.0),
        ],
    )
    msgs += [send(snd_v.at[0:4], rcv_v.at[0:4], (partner, gy))]
    launch()
    own_a = with_terms(half(swap(pick(mid, by_side(um, up))), True), terms[0])
    own_b = swap(pick(op, o_sum))
    own_c = pick(om, 0.0)

    def got(at):
        return rcv_v[at].astype(F32)

    def spread(end, at):
        first, second = rcy_v[end, at].astype(F32), rcy_v[end, at + 1].astype(F32)
        code = jnp.broadcast_to(first[:, 112:113], (32, 128))
        results = []
        for tile in (first, second):
            rows = []
            for a in range(AGG):
                here = jnp.where(code == float(a), tile, 0.0)
                rows.append(here[0:8] + here[8:16] + here[16:24] + here[24:32])
            results.append(jnp.concatenate(rows, axis=0))
        return results

    await_all(msgs[6:7])
    own_a, far_a = own_a + got(3), far_a + got(0)
    far_b, far_c = far_b + got(1), far_c + got(2)
    await_all(msgs[2:4])
    (near_a, near_b), (past_a, past_b) = spread(1, 0), spread(1, 2)
    own_a, own_b = own_a + near_a, own_b + near_b
    far_a, far_b = far_a + past_a, far_b + past_b
    await_all(msgs[4:6])
    own_a, own_b, own_c = own_a + got(4), own_b + got(5), own_c + got(6)
    far_a = far_a + got(7)
    await_all(msgs[0:2])
    (near_a, near_b), (past_a, past_b) = spread(0, 0), spread(0, 2)
    own_a, own_b = own_a + near_a, own_b + pick(near_b, 0.0)
    own_c = own_c + pick(swap(near_b), 0.0)
    far_a, far_b = far_a + past_a, far_b + pick(past_b, 0.0)
    far_c = far_c + pick(swap(past_b), 0.0)

    def both(own, far):
        first, second = jnp.where(is_odd, far, own), jnp.where(is_odd, own, far)
        return jnp.concatenate([first, second], axis=0).T

    a, b, c = both(own_a, far_a), both(own_b, far_b), both(own_c, far_c)

    @pl.when(odd == 0)
    def _():
        out[128:192] = c[64:128]
        out[320:384] = c[0:64]
        out[384:512] = b
        out[704:800] = a[0:96]
        out[800:801] = a[96:97] + a[97:98]

    @pl.when(odd == 1)
    def _():
        out[0:32] = a[64:96]
        out[32:96] = a[0:64]
        out[288:352] = c[0:64]
        out[352:480] = b
        out[608:672] = c[64:128]
        out[800:801] = swap(a[96:97] + a[97:98])

    together(sends, lambda copy: copy.wait_send())


def finish_kernel(data, coarse, restricted, row, sem):
    first = pltpu.make_async_copy(data.at[pl.ds(0, 800)], coarse.at[0, 0], sem.at[0])
    first.start()
    row[...] = data[800:801, 0:64]
    second = pltpu.make_async_copy(row, restricted.at[0], sem.at[1])
    second.start()
    first.wait()
    second.wait()


def body(stencil, inverse, tentative, aggregate, residual):
    hbm = pl.BlockSpec(memory_space=pltpu.HBM)
    aggregate = aggregate.transpose(0, 2, 1)
    operands = [
        pltpu.with_memory_space_constraint(operand, pltpu.HBM)
        for operand in (stencil, inverse, tentative, aggregate, residual)
    ]
    vmem = pl.BlockSpec(memory_space=pltpu.VMEM)
    scratch = [
        pltpu.VMEM(stencil.shape, BF16),
        pltpu.VMEM(inverse.shape, BF16),
        pltpu.VMEM(tentative.shape, BF16),
        pltpu.VMEM(aggregate.shape, jnp.int32),
        pltpu.VMEM(residual.shape, F32),
        pltpu.VMEM((4, 4, 256, 256), BF16),
        pltpu.VMEM((4, 256, 256), BF16),
        pltpu.VMEM((2, 4, 16, 128), BF16),
        pltpu.VMEM((2, 4, 16, 128), BF16),
        pltpu.VMEM((2, 2, 16, 128), BF16),
        pltpu.VMEM((2, 2, 16, 128), BF16),
        pltpu.VMEM((6, 64, 256), BF16),
        pltpu.VMEM((6, 64, 256), BF16),
        pltpu.VMEM((2, 2, 64, 256), BF16),
        pltpu.VMEM((4, 64, 256), BF16),
        pltpu.VMEM((4, 64, 256), BF16),
        pltpu.VMEM((2, 64, 256), BF16),
        pltpu.VMEM((4, 64, 256), BF16),
        pltpu.VMEM((4, 192, 256), BF16),
        pltpu.VMEM((4, 256, 256), F32),
        pltpu.VMEM((8, 64, 128), BF16),
        pltpu.VMEM((8, 64, 128), BF16),
        pltpu.VMEM((2, 4, 32, 128), BF16),
        pltpu.VMEM((2, 4, 32, 128), BF16),
        pltpu.SemaphoreType.DMA((10,)),
        pltpu.SemaphoreType.DMA((23,)),
        pltpu.SemaphoreType.DMA((23,)),
    ]
    sizes = (lax.axis_size("gx"), lax.axis_size("gy"))

    def call(*refs):
        kernel(*sizes, *refs)

    coarse = pl.pallas_call(
        call,
        out_shape=pltpu.VMEM((808, 128), F32),
        in_specs=[hbm] * 5,
        out_specs=vmem,
        scratch_shapes=scratch,
        compiler_params=pltpu.CompilerParams(
            collective_id=0, has_side_effects=True, vmem_limit_bytes=32 << 20
        ),
        name="galerkin",
    )(*operands)
    coarse, restricted = pl.pallas_call(
        finish_kernel,
        out_shape=(
            jax.ShapeDtypeStruct((1, 1, 800, 128), F32),
            jax.ShapeDtypeStruct((1, 1, 64), F32),
        ),
        in_specs=[pl.BlockSpec(memory_space=pltpu.VMEM)],
        out_specs=(pl.BlockSpec(memory_space=pl.ANY), pl.BlockSpec(memory_space=pl.ANY)),
        scratch_shapes=[pltpu.VMEM((1, 64), F32), pltpu.SemaphoreType.DMA((2,))],
        name="store",
    )(pltpu.with_memory_space_constraint(coarse, pltpu.VMEM))
    return coarse.swapaxes(2, 3), restricted


def solution(mesh):
    in_specs = (
        P("gx", "gy", None, None, None),
        P("gx", "gy", None, None),
        P("gx", "gy", None, None),
        P("gx", "gy", None),
        P("gx", "gy", None),
    )
    out_specs = (P("gx", "gy", None, None), P("gx", "gy", None))
    return jax.shard_map(body, mesh=mesh, in_specs=in_specs, out_specs=out_specs, check_vma=False)
```
